32 devices in a mesh: row: 8 (over z, x), col: 4 (over y, core).
Axes of the slice: x: 2, y: 2, z: 4, core: 2. Of those that a mesh axis runs over, the one named last changes fastest.
Arguments:
- initial_heat: bfloat16 [48, 256, 1024], P(None, 'row', 'col'), may hold values from -6 to 6
- layer_conductance: bfloat16 [47, 256, 1024], P(None, 'row', 'col'), may hold values from 0.049804688 to 20
- layer_spacing: float32 [48], replicated, may hold values from 0.5 to 2
- submerged_layers: int32 [256, 1024], P('row', 'col'), may hold values from 1 to 48
- water_indicator: int32 [256, 1024], P('row', 'col'), may hold values from 0 to 1, as said below
- seafloor_distance: float32 [256, 1024], P('row', 'col'), may hold values from 0.5 to 2
Outputs:
- diffused_heat: float32 [48, 256, 1024], P(None, 'row', 'col')
- height: float32 [256, 1024], P('row', 'col')
The draws below stay inside these ranges and needn't reach their ends.
Inputs may be any that keep to these rules, and one draw needn't show every extreme that they name: `water_indicator`: land lies in a few large regions and in scattered single cells.
All inputs are finite; a program needn't handle non-finite values.
Results may differ from the reference program's by a relative error of at most 0.0003.
Values sent between devices are 32-bit elements; how exact they have to be, the bound alone decides.
A program may use at most 64 MiB of HBM per device.

```python
import math
import jax
import jax.numpy as jnp
from jax import lax

DEPTH_LAYERS = 48
PATCH_NORTH_SOUTH = 32
ITERS = 4
MESH_NORTH_SOUTH = 256
MESH_EAST_WEST = 1024
N_ROW = 8


def draw_water_indicator(key, part):
    region_count = 6
    keys = jax.random.split(jax.random.fold_in(key, 7331), 5)
    lat_start = jax.random.randint(keys[0], (region_count,), 0, MESH_NORTH_SOUTH)
    lon_start = jax.random.randint(keys[1], (region_count,), 0, MESH_EAST_WEST)
    lat_span = jax.random.randint(keys[2], (region_count,), MESH_NORTH_SOUTH // 16 + 1, MESH_NORTH_SOUTH // 4 + 2)
    lon_span = jax.random.randint(keys[3], (region_count,), MESH_EAST_WEST // 16 + 1, MESH_EAST_WEST // 4 + 2)
    lat_index = jnp.arange(MESH_NORTH_SOUTH, dtype=jnp.int32)
    lon_index = jnp.arange(MESH_EAST_WEST, dtype=jnp.int32)
    inside_lat = (lat_index[None, :] >= lat_start[:, None]) & (lat_index[None, :] < lat_start[:, None] + lat_span[:, None])
    lon_offset = (lon_index[None, :] - lon_start[:, None]) % MESH_EAST_WEST
    inside_lon = lon_offset < lon_span[:, None]
    land = jnp.any(inside_lat[:, :, None] & inside_lon[:, None, :], axis=0)
    scattered = jax.random.randint(keys[4], (MESH_NORTH_SOUTH, MESH_EAST_WEST), 0, 10) == 0
    return jnp.where(land | scattered, 0, 1).astype(jnp.int32)


def set_ends(values, own_key, least, high):
    extent = values.shape
    place = [jax.random.randint(jax.random.fold_in(own_key, axis), (), 0, extent[axis]) for axis in range(len(extent))]
    values = values.at[tuple(place)].set(least)
    longest = extent.index(max(extent))
    place[longest] = (place[longest] + 1) % extent[longest]
    return values.at[tuple(place)].set(high)


def level_of(own_key, extent, shards, low, largest):
    def one(position, blocks):
        steps = jax.random.uniform(jax.random.fold_in(jax.random.fold_in(own_key, 6), position), (blocks,), jnp.float32, low / len(shards), largest / len(shards))
        return jnp.repeat(jnp.exp(steps), extent[position] // blocks).reshape((-1,) + (1,) * (len(extent) - position - 1))

    factor_of = one(*shards[0])
    for cut in shards[1:]:
        factor_of = factor_of * one(*cut)
    return factor_of


def normal_values(key, extent, deviation, most, pieces=(), kind=jnp.bfloat16):
    gain = level_of(key, extent, pieces, -0.22, 0.18) if pieces else 1.0
    array = jax.random.normal(key, extent, jnp.float32) * deviation * gain
    return jnp.minimum(jnp.maximum(array, -most), most).astype(kind)


def setup_inputs(seed: int = 0) -> dict:
    key_of = jax.random.split(jax.random.key(seed), 7)
    initial_heat = normal_values(key_of[0], (DEPTH_LAYERS, MESH_NORTH_SOUTH, MESH_EAST_WEST), 1.0, 6.0, ((1, 8), (2, 4)))
    layer_conductance = jnp.clip(jnp.exp(math.log(20.0) - 5.9953784 * jax.random.uniform(key_of[1], (DEPTH_LAYERS - 1, MESH_NORTH_SOUTH, MESH_EAST_WEST), jnp.float32) ** level_of(key_of[1], (DEPTH_LAYERS - 1, MESH_NORTH_SOUTH, MESH_EAST_WEST), ((1, 8), (2, 4)), -0.2, 0.2)), 0.049804688, 20.0).astype(jnp.bfloat16)
    layer_spacing = jnp.clip(jnp.exp(jax.random.uniform(key_of[2], (DEPTH_LAYERS,), jnp.float32, math.log(0.5), math.log(2.0))), 0.5, 2.0)
    submerged_layers = set_ends(jax.random.randint(key_of[3], (MESH_NORTH_SOUTH, MESH_EAST_WEST), 1, DEPTH_LAYERS + 1), jax.random.fold_in(key_of[3], 1), 1, DEPTH_LAYERS).astype(jnp.int32)
    water_indicator = draw_water_indicator(jax.random.fold_in(key_of[6], 71), 0)
    seafloor_distance = jnp.clip(jnp.exp(math.log(2.0) - 1.3862944 * jax.random.uniform(key_of[5], (MESH_NORTH_SOUTH, MESH_EAST_WEST), jnp.float32) ** level_of(key_of[5], (MESH_NORTH_SOUTH, MESH_EAST_WEST), ((0, 8), (1, 4)), -0.2, 0.2)), 0.5, 2.0)
    return {"initial_heat": initial_heat, "layer_conductance": layer_conductance, "layer_spacing": layer_spacing, "submerged_layers": submerged_layers, "water_indicator": water_indicator, "seafloor_distance": seafloor_distance}


surface_term = 0.5
compass = ((-1, -1, 0.5), (-1, 0, 1.0), (-1, 1, 0.5), (0, -1, 1.0), (0, 1, 1.0), (1, -1, 0.5), (1, 0, 1.0), (1, 1, 0.5))

def backward_euler_vertical_diffuse(initial_heat, layer_conductance, layer_spacing, submerged_layers):
    layer_pile = initial_heat.shape[0]
    index = jnp.arange(layer_pile - 1, dtype=jnp.int32)
    couple = layer_conductance.astype(jnp.float32) * (index[:, None, None] + 1 < submerged_layers[None]).astype(jnp.float32)
    zero_level = jnp.zeros((1,) + submerged_layers.shape, jnp.float32)
    below = jnp.concatenate([zero_level, couple], axis=0)
    above = jnp.concatenate([couple, zero_level], axis=0)
    spacing_profile = layer_spacing[:, None, None]
    driving_term = spacing_profile * initial_heat.astype(jnp.float32)
    centre = spacing_profile + below + above

    def forward(carry, level):
        ratio_prev, value_prev = carry
        lower_level, upper_level, centre_level, source_level = level
        pivot = centre_level - lower_level * ratio_prev
        ratio = upper_level / pivot
        value = (source_level + lower_level * value_prev) / pivot
        return ((ratio, value), (ratio, value))
    start = (jnp.zeros(submerged_layers.shape, jnp.float32), jnp.zeros(submerged_layers.shape, jnp.float32))
    unused, (ratios, values) = lax.scan(forward, start, (below, above, centre, driving_term))

    def backward(carry, level):
        ratio, value = level
        result = value + ratio * carry
        return (result, result)
    unused, diffused_heat = lax.scan(backward, jnp.zeros(submerged_layers.shape, jnp.float32), (ratios, values), reverse=True)
    return diffused_heat

def depth_forcing(diffused_heat, layer_spacing, submerged_layers, water_indicator):
    layer_pile = diffused_heat.shape[0]
    index = jnp.arange(layer_pile, dtype=jnp.int32)
    live = (index[:, None, None] < submerged_layers[None]).astype(jnp.float32)
    total = lax.optimization_barrier(jnp.sum(layer_spacing[:, None, None] * live * diffused_heat, axis=0))
    return water_indicator.astype(jnp.float32) * total / math.sqrt(layer_pile)

def neighbour(field, offset_row, offset_col, first, count):
    return jnp.roll(field[first + offset_row:first + offset_row + count], -offset_col, axis=1)

def couplings(height_field, ocean_field, first, count):
    here_height = height_field[first:first + count]
    here_ocean = ocean_field[first:first + count]
    weights = []
    for offset_row, offset_col, factor in compass:
        other_height = neighbour(height_field, offset_row, offset_col, first, count)
        other_ocean = neighbour(ocean_field, offset_row, offset_col, first, count)
        weights.append(factor * here_ocean * other_ocean * (0.5 * (here_height + other_height)))
    weights = jnp.stack(weights)
    return (weights, surface_term + lax.optimization_barrier(jnp.sum(weights, axis=0)))

def operate(field, weights, centre, first, count):
    result = centre * field[first:first + count]
    for slot, (offset_row, offset_col, factor) in enumerate(compass):
        result = result - weights[slot] * neighbour(field, offset_row, offset_col, first, count)
    return result

def chebyshev_scalars(top):
    theta = 0.5 * (top + surface_term)
    delta = 0.5 * (top - surface_term)
    return (theta, delta, theta / delta)

def reference(initial_heat, layer_conductance, layer_spacing, submerged_layers, water_indicator, seafloor_distance):

    def each_patch(block):
        temp_block, diff_block, wet_block, mask_block = block
        mixed_block = backward_euler_vertical_diffuse(temp_block, diff_block, layer_spacing, wet_block)
        return (mixed_block, depth_forcing(mixed_block, layer_spacing, wet_block, mask_block))
    heat_patches = jnp.moveaxis(initial_heat.reshape(DEPTH_LAYERS, N_ROW, PATCH_NORTH_SOUTH, MESH_EAST_WEST), 1, 0)
    diffusion_patches = jnp.moveaxis(layer_conductance.reshape(DEPTH_LAYERS - 1, N_ROW, PATCH_NORTH_SOUTH, MESH_EAST_WEST), 1, 0)
    diffused_patches, driving_patches = lax.map(each_patch, (heat_patches, diffusion_patches, submerged_layers.reshape(N_ROW, PATCH_NORTH_SOUTH, MESH_EAST_WEST), water_indicator.reshape(N_ROW, PATCH_NORTH_SOUTH, MESH_EAST_WEST)))
    diffused_heat = jnp.moveaxis(diffused_patches, 0, 1).reshape(DEPTH_LAYERS, MESH_NORTH_SOUTH, MESH_EAST_WEST)
    forcing = driving_patches.reshape(MESH_NORTH_SOUTH, MESH_EAST_WEST)
    height_pad = jnp.pad(seafloor_distance, ((1, 1), (0, 0)))
    ocean_pad = jnp.pad(water_indicator.astype(jnp.float32), ((1, 1), (0, 0)))
    weights, centre = couplings(height_pad, ocean_pad, 1, MESH_NORTH_SOUTH)
    top = jnp.max(2.0 * centre - surface_term)
    theta, delta, sigma = chebyshev_scalars(top)
    solution = jnp.zeros_like(forcing)
    residual = forcing
    direction = forcing / theta
    recur = 1.0 / sigma
    for step in range(ITERS):
        solution = solution + direction
        image = operate(jnp.pad(direction, ((1, 1), (0, 0))), weights, centre, 1, MESH_NORTH_SOUTH)
        residual = residual - image
        recur_next = 1.0 / (2.0 * sigma - recur)
        direction = recur_next * recur * direction + 2.0 * recur_next / delta * residual
        recur = recur_next
    return (diffused_heat, solution + direction)
```

```python
import functools
import math

import jax
import jax.numpy as jnp
from jax import lax
from jax.experimental import pallas as pl
from jax.experimental.pallas import tpu as pltpu
from jax.sharding import PartitionSpec as P

ITERS = 4
SURFACE = 0.5
MESH = pl.DeviceIdType.MESH
GROUP = 4
SLOT = 8


def spread(field):
    rows, lanes = field.shape
    t = pltpu.roll(field, 1, 0) + pltpu.roll(field, rows - 1, 0)
    h = field + 0.5 * t
    return t + (pltpu.roll(h, 1, 1) + pltpu.roll(h, lanes - 1, 1))


def shift(block, by):
    lanes = block.shape[1]
    by = by % lanes
    return block if by == 0 else pltpu.roll(block, by, 1)


def kernel(
    n_row,
    n_col,
    heat_hbm,
    cond_hbm,
    spacing,
    wet_ref,
    water_ref,
    depth_ref,
    out_hbm,
    height_ref,
    heat,
    cond,
    ratios,
    values,
    ext,
    top_stage,
    bot_stage,
    west_stage,
    east_stage,
    land_n,
    land_s,
    land_w,
    land_e,
    land_c,
    col_max,
    row_max,
    in_sem,
    out_sem,
    send_sem,
    recv_sem,
    col_send,
    col_recv,
    row_send,
    row_recv,
):
    levels, rows, cols = heat.shape
    half = cols - 128
    row, col = lax.axis_index("row"), lax.axis_index("col")
    north, south = row > 0, row < n_row - 1
    up, down = lax.rem(row + n_row - 1, n_row), lax.rem(row + 1, n_row)
    west, east = lax.rem(col + n_col - 1, n_col), lax.rem(col + 1, n_col)

    get_heat = pltpu.make_async_copy(heat_hbm, heat, in_sem.at[0])
    get_cond = pltpu.make_async_copy(cond_hbm, cond, in_sem.at[1])
    get_heat.start()
    get_cond.start()

    barrier = pltpu.get_barrier_semaphore()

    def greet(r, c):
        pl.semaphore_signal(barrier, inc=1, device_id=(r, c), device_id_type=MESH)

    for off in range(1, n_col):
        greet(row, lax.rem(col + off, n_col))
    for off in range(1, n_row):
        greet(lax.rem(row + off, n_row), col)

    @pl.when(north)
    def _():
        greet(up, west)
        greet(up, east)

    @pl.when(south)
    def _():
        greet(down, west)
        greet(down, east)

    @pl.when(jnp.logical_not(north))
    def _():
        land_n[...] = jnp.zeros_like(land_n)
        land_c[0] = jnp.zeros_like(land_c[0])
        land_c[1] = jnp.zeros_like(land_c[1])

    @pl.when(jnp.logical_not(south))
    def _():
        land_s[...] = jnp.zeros_like(land_s)
        land_c[2] = jnp.zeros_like(land_c[2])
        land_c[3] = jnp.zeros_like(land_c[3])

    wet = wet_ref[...]
    mask = water_ref[...].astype(jnp.float32)
    masked_depth = mask * depth_ref[...]
    get_heat.wait()

    def add_levels(step, total):
        for j in range(GROUP):
            k = step * GROUP + j
            total = total + jnp.where(k < wet, spacing[k] * heat[k].astype(jnp.float32), 0.0)
        return total

    total = lax.fori_loop(0, levels // GROUP, add_levels, jnp.zeros((rows, cols), jnp.float32))
    forcing = mask * total / math.sqrt(levels)

    fields = (masked_depth, mask, forcing)
    for slot, field in enumerate(fields):
        ext[slot, :rows, :cols] = field
    sub8 = lax.broadcasted_iota(jnp.int32, (8, cols), 0)
    top_stage[0:8] = jnp.where(sub8 < 4, masked_depth[:8], pltpu.roll(mask[:8], 4, 0))
    top_stage[8:16] = forcing[:8]
    bot_stage[0:8] = jnp.where(sub8 >= 4, masked_depth[rows - 8 :], pltpu.roll(mask[rows - 8 :], 4, 0))
    bot_stage[8:16] = forcing[rows - 8 :]
    lane = lax.broadcasted_iota(jnp.int32, (rows, 128), 1)
    west_stage[...] = jnp.where(
        lane < SLOT,
        masked_depth[:, :128],
        jnp.where(lane < 2 * SLOT, shift(mask[:, :128], SLOT), shift(forcing[:, :128], 2 * SLOT)),
    )
    east_stage[...] = jnp.where(
        lane >= 128 - SLOT,
        masked_depth[:, half:],
        jnp.where(
            lane >= 128 - 2 * SLOT, shift(mask[:, half:], -SLOT), shift(forcing[:, half:], -2 * SLOT)
        ),
    )

    def remote(src, dst, slot, target):
        return pltpu.make_async_remote_copy(
            src_ref=src,
            dst_ref=dst,
            send_sem=send_sem.at[slot],
            recv_sem=recv_sem.at[slot],
            device_id=target,
            device_id_type=MESH,
        )

    low, high = pl.ds(0, 8), pl.ds(rows - 8, 8)
    to_n = remote(top_stage, land_s, 0, (up, col))
    to_s = remote(bot_stage, land_n, 1, (down, col))
    to_w = remote(west_stage, land_e, 2, (row, west))
    to_e = remote(east_stage, land_w, 3, (row, east))
    to_nw = remote(west_stage.at[low], land_c.at[3], 4, (up, west))
    to_ne = remote(east_stage.at[low], land_c.at[2], 5, (up, east))
    to_sw = remote(west_stage.at[high], land_c.at[1], 6, (down, west))
    to_se = remote(east_stage.at[high], land_c.at[0], 7, (down, east))
    northward, southward, sideways = (to_n, to_nw, to_ne), (to_s, to_sw, to_se), (to_w, to_e)

    diagonal = 2 * (north.astype(jnp.int32) + south.astype(jnp.int32))
    pl.semaphore_wait(barrier, n_row + n_col - 2 + diagonal)

    @pl.when(north)
    def _():
        for copy in northward:
            copy.start()

    @pl.when(south)
    def _():
        for copy in southward:
            copy.start()

    for copy in sideways:
        copy.start()

    get_cond.wait()

    def eliminate(k, carry):
        ratio, value, above, source, coupling = carry
        spread_out = spacing[k] + coupling + above * (1.0 - ratio)
        inverse = 1.0 / spread_out
        ratio = coupling * inverse
        value = (source + above * value) * inverse
        ratios[k] = ratio
        values[k] = value
        return ratio, value

    def forward(step, carry):
        ratio, value, above = carry
        for j in range(GROUP):
            k = step * GROUP + j
            coupling = jnp.where(k + 1 < wet, cond[k].astype(jnp.float32), 0.0)
            source = spacing[k] * heat[k].astype(jnp.float32)
            ratio, value = eliminate(k, (ratio, value, above, source, coupling))
            above = coupling
        return ratio, value, above

    zero = jnp.zeros((rows, cols), jnp.float32)
    whole = (levels - 1) // GROUP
    ratio, value, above = lax.fori_loop(0, whole, forward, (zero, zero, zero))
    for k in range(whole * GROUP, levels):
        source = spacing[k] * heat[k].astype(jnp.float32)
        if k < levels - 1:
            coupling = jnp.where(k + 1 < wet, cond[k].astype(jnp.float32), 0.0)
        else:
            coupling = zero
        ratio, value = eliminate(k, (ratio, value, above, source, coupling))
        above = coupling

    @pl.when(south)
    def _():
        for copy in northward:
            copy.wait_recv()

    @pl.when(north)
    def _():
        for copy in southward:
            copy.wait_recv()

    for copy in sideways:
        copy.wait_recv()

    from_n, from_s = land_n[...], land_s[...]
    ext[0, rows:, :cols] = jnp.where(sub8 < 4, from_s[:8], from_n[:8])
    ext[1, rows:, :cols] = pltpu.roll(jnp.where(sub8 >= 4, from_s[:8], from_n[:8]), 4, 0)
    ext[2, rows:, :cols] = jnp.where(sub8 < 4, from_s[8:], from_n[8:])
    sub_c = lax.broadcasted_iota(jnp.int32, (8, 128), 0)
    east_side = jnp.concatenate([land_e[...], jnp.where(sub_c < 4, land_c[3], land_c[1])], axis=0)
    west_side = jnp.concatenate([land_w[...], jnp.where(sub_c < 4, land_c[2], land_c[0])], axis=0)
    lane_x = lax.broadcasted_iota(jnp.int32, (rows + 8, 128), 1)
    for slot in range(3):
        ext[slot, :, cols:] = jnp.where(
            lane_x < 64, shift(east_side, -SLOT * slot), shift(west_side, SLOT * slot)
        )

    e, m = ext[0], ext[1]
    half_e, half_m = 0.5 * e, 0.5 * m
    centre = SURFACE + (half_e * spread(m) + half_m * spread(e))
    bound = 2.0 * centre[:rows, :cols] - SURFACE
    bound = jnp.max(bound, axis=0, keepdims=True)
    local = bound[:, :128]
    for start in range(128, cols, 128):
        local = jnp.maximum(local, bound[:, start : start + 128])
    col_max[0] = local

    def tell(buffer, off, sends, recvs, target):
        return pltpu.make_async_remote_copy(
            src_ref=buffer.at[0],
            dst_ref=buffer.at[off],
            send_sem=sends.at[off],
            recv_sem=recvs.at[off],
            device_id=target,
            device_id_type=MESH,
        )

    col_tells = [
        tell(col_max, off, col_send, col_recv, (row, lax.rem(col + off, n_col)))
        for off in range(1, n_col)
    ]
    row_tells = [
        tell(row_max, off, row_send, row_recv, (lax.rem(row + off, n_row), col))
        for off in range(1, n_row)
    ]
    for copy in col_tells:
        copy.start()

    parts = out_sem.shape[0]
    per = levels // parts

    def backward_part(part, carry):
        def backward(step, carry):
            for j in range(GROUP):
                k = (part + 1) * per - 1 - (step * GROUP + j)
                carry = values[k] + ratios[k] * carry
                values[k] = carry
            return carry

        carry = lax.fori_loop(0, per // GROUP, backward, carry)
        put = pltpu.make_async_copy(
            values.at[pl.ds(part * per, per)], out_hbm.at[pl.ds(part * per, per)], out_sem.at[part]
        )
        put.start()
        return carry, put

    carry = zero
    puts = []
    for part in reversed(range(parts // 2, parts)):
        carry, put = backward_part(part, carry)
        puts.append(put)

    for copy in col_tells:
        copy.wait_recv()
    best = col_max[0]
    for off in range(1, n_col):
        best = jnp.maximum(best, col_max[off])
    row_max[0] = best
    for copy in row_tells:
        copy.start()

    for part in reversed(range(parts // 2)):
        carry, put = backward_part(part, carry)
        puts.append(put)

    for copy in row_tells:
        copy.wait_recv()
    best = row_max[0]
    for off in range(1, n_row):
        best = jnp.maximum(best, row_max[off])
    top = jnp.max(best, axis=1, keepdims=True)

    theta = 0.5 * (top + SURFACE)
    delta = 0.5 * (top - SURFACE)
    sigma = theta / delta
    residual = ext[2]
    direction = residual * (1.0 / theta)
    recur = 1.0 / sigma
    result = jnp.zeros_like(residual)
    for _ in range(ITERS):
        result = result + direction
        image = centre * direction - (
            half_e * spread(m * direction) + half_m * spread(e * direction)
        )
        residual = residual - image
        recur_next = 1.0 / (2.0 * sigma - recur)
        direction = (recur_next * recur) * direction + (2.0 * recur_next / delta) * residual
        recur = recur_next
    height_ref[...] = (result + direction)[:rows, :cols]

    @pl.when(north)
    def _():
        for copy in northward:
            copy.wait_send()

    @pl.when(south)
    def _():
        for copy in southward:
            copy.wait_send()

    for copy in sideways + tuple(col_tells) + tuple(row_tells):
        copy.wait_send()
    for put in puts:
        put.wait()


def local(n_row, n_col, heat, cond, spacing, wet, water, depth):
    levels, rows, cols = heat.shape
    f32 = jnp.float32
    parts = 4
    vmem = pl.BlockSpec(memory_space=pltpu.VMEM)
    hbm = pl.BlockSpec(memory_space=pl.ANY)
    dma = pltpu.SemaphoreType.DMA
    return pl.pallas_call(
        functools.partial(kernel, n_row, n_col),
        out_shape=(
            jax.ShapeDtypeStruct((levels, rows, cols), f32),
            jax.ShapeDtypeStruct((rows, cols), f32),
        ),
        in_specs=[hbm, hbm, pl.BlockSpec(memory_space=pltpu.SMEM), vmem, vmem, vmem],
        out_specs=(hbm, vmem),
        scratch_shapes=[
            pltpu.VMEM((levels, rows, cols), heat.dtype),
            pltpu.VMEM((levels - 1, rows, cols), cond.dtype),
            pltpu.VMEM((levels, rows, cols), f32),
            pltpu.VMEM((levels, rows, cols), f32),
            pltpu.VMEM((3, rows + 8, cols + 128), f32),
            pltpu.VMEM((16, cols), f32),
            pltpu.VMEM((16, cols), f32),
            pltpu.VMEM((rows, 128), f32),
            pltpu.VMEM((rows, 128), f32),
            pltpu.VMEM((16, cols), f32),
            pltpu.VMEM((16, cols), f32),
            pltpu.VMEM((rows, 128), f32),
            pltpu.VMEM((rows, 128), f32),
            pltpu.VMEM((4, 8, 128), f32),
            pltpu.VMEM((n_col, 1, 128), f32),
            pltpu.VMEM((n_row, 1, 128), f32),
            dma((2,)),
            dma((parts,)),
            dma((8,)),
            dma((8,)),
            dma((n_col,)),
            dma((n_col,)),
            dma((n_row,)),
            dma((n_row,)),
        ],
        compiler_params=pltpu.CompilerParams(
            collective_id=0, has_side_effects=True, vmem_limit_bytes=32 * 1024 * 1024
        ),
    )(heat, cond, spacing, wet, water, depth)


def solution(mesh):
    placed = (
        P(None, "row", "col"),
        P(None, "row", "col"),
        P(),
        P("row", "col"),
        P("row", "col"),
        P("row", "col"),
    )
    return jax.shard_map(
        functools.partial(local, mesh.shape["row"], mesh.shape["col"]),
        mesh=mesh,
        in_specs=placed,
        out_specs=(P(None, "row", "col"), P("row", "col")),
        check_vma=False,
    )
```

```python
import functools
import math

import jax
import jax.numpy as jnp
from jax import lax
from jax.experimental import pallas as pl
from jax.experimental.pallas import tpu as pltpu
from jax.sharding import PartitionSpec as P

ITERS = 4
SURFACE = 0.5
MESH = pl.DeviceIdType.MESH
GROUP = 4
GRANT = 60 * 1024 * 1024
SLOT = 8


def spread(field):
    rows, lanes = field.shape
    t = pltpu.roll(field, 1, 0) + pltpu.roll(field, rows - 1, 0)
    h = field + 0.5 * t
    return t + (pltpu.roll(h, 1, 1) + pltpu.roll(h, lanes - 1, 1))


def shift(block, by):
    lanes = block.shape[1]
    by = by % lanes
    return block if by == 0 else pltpu.roll(block, by, 1)


def kernel(
    n_row,
    n_col,
    heat_hbm,
    cond_hbm,
    spacing_hbm,
    wet_hbm,
    water_hbm,
    depth_hbm,
    out_hbm,
    height_hbm,
    heat,
    cond,
    spacing,
    wet_ref,
    water_ref,
    depth_ref,
    ratios,
    values,
    height_ref,
    ext,
    top_stage,
    bot_stage,
    west_stage,
    east_stage,
    land_n,
    land_s,
    land_w,
    land_e,
    land_c,
    col_max,
    row_max,
    in_sem,
    out_sem,
    send_sem,
    recv_sem,
    col_send,
    col_recv,
    row_send,
    row_recv,
):
    levels, rows, cols = heat.shape
    half = cols - 128
    row, col = lax.axis_index("row"), lax.axis_index("col")
    north, south = row > 0, row < n_row - 1
    up, down = lax.rem(row + n_row - 1, n_row), lax.rem(row + 1, n_row)
    west, east = lax.rem(col + n_col - 1, n_col), lax.rem(col + 1, n_col)

    pairs = (
        (wet_hbm, wet_ref),
        (spacing_hbm, spacing),
        (water_hbm, water_ref),
        (depth_hbm, depth_ref),
        (heat_hbm, heat),
        (cond_hbm, cond),
    )
    gets = [pltpu.make_async_copy(a, b, in_sem.at[i]) for i, (a, b) in enumerate(pairs)]
    for get in gets:
        get.start()
    get_cond = gets.pop()

    barrier = pltpu.get_barrier_semaphore()

    def greet(r, c):
        pl.semaphore_signal(barrier, inc=1, device_id=(r, c), device_id_type=MESH)

    for off in range(1, n_col):
        greet(row, lax.rem(col + off, n_col))
    for off in range(1, n_row):
        greet(lax.rem(row + off, n_row), col)

    @pl.when(north)
    def _():
        greet(up, west)
        greet(up, east)

    @pl.when(south)
    def _():
        greet(down, west)
        greet(down, east)

    @pl.when(jnp.logical_not(north))
    def _():
        land_n[...] = jnp.zeros_like(land_n)
        land_c[0] = jnp.zeros_like(land_c[0])
        land_c[1] = jnp.zeros_like(land_c[1])

    @pl.when(jnp.logical_not(south))
    def _():
        land_s[...] = jnp.zeros_like(land_s)
        land_c[2] = jnp.zeros_like(land_c[2])
        land_c[3] = jnp.zeros_like(land_c[3])

    for get in gets:
        get.wait()
    wet = wet_ref[...]
    mask = water_ref[...].astype(jnp.float32)
    masked_depth = mask * depth_ref[...]

    def add_levels(step, total):
        for j in range(GROUP):
            k = step * GROUP + j
            total = total + jnp.where(k < wet, spacing[k] * heat[k].astype(jnp.float32), 0.0)
        return total

    total = lax.fori_loop(0, levels // GROUP, add_levels, jnp.zeros((rows, cols), jnp.float32))
    forcing = mask * total / math.sqrt(levels)

    fields = (masked_depth, mask, forcing)
    for slot, field in enumerate(fields):
        ext[slot, :rows, :cols] = field
    sub8 = lax.broadcasted_iota(jnp.int32, (8, cols), 0)
    top_stage[0:8] = jnp.where(sub8 < 4, masked_depth[:8], pltpu.roll(mask[:8], 4, 0))
    top_stage[8:16] = forcing[:8]
    bot_stage[0:8] = jnp.where(sub8 >= 4, masked_depth[rows - 8 :], pltpu.roll(mask[rows - 8 :], 4, 0))
    bot_stage[8:16] = forcing[rows - 8 :]
    lane = lax.broadcasted_iota(jnp.int32, (rows, 128), 1)
    west_stage[...] = jnp.where(
        lane < SLOT,
        masked_depth[:, :128],
        jnp.where(lane < 2 * SLOT, shift(mask[:, :128], SLOT), shift(forcing[:, :128], 2 * SLOT)),
    )
    east_stage[...] = jnp.where(
        lane >= 128 - SLOT,
        masked_depth[:, half:],
        jnp.where(
            lane >= 128 - 2 * SLOT, shift(mask[:, half:], -SLOT), shift(forcing[:, half:], -2 * SLOT)
        ),
    )

    def remote(src, dst, slot, target):
        return pltpu.make_async_remote_copy(
            src_ref=src,
            dst_ref=dst,
            send_sem=send_sem.at[slot],
            recv_sem=recv_sem.at[slot],
            device_id=target,
            device_id_type=MESH,
        )

    low, high = pl.ds(0, 8), pl.ds(rows - 8, 8)
    to_n = remote(top_stage, land_s, 0, (up, col))
    to_s = remote(bot_stage, land_n, 1, (down, col))
    to_w = remote(west_stage, land_e, 2, (row, west))
    to_e = remote(east_stage, land_w, 3, (row, east))
    to_nw = remote(west_stage.at[low], land_c.at[3], 4, (up, west))
    to_ne = remote(east_stage.at[low], land_c.at[2], 5, (up, east))
    to_sw = remote(west_stage.at[high], land_c.at[1], 6, (down, west))
    to_se = remote(east_stage.at[high], land_c.at[0], 7, (down, east))
    northward, southward, sideways = (to_n, to_nw, to_ne), (to_s, to_sw, to_se), (to_w, to_e)

    diagonal = 2 * (north.astype(jnp.int32) + south.astype(jnp.int32))
    pl.semaphore_wait(barrier, n_row + n_col - 2 + diagonal)

    @pl.when(north)
    def _():
        for copy in northward:
            copy.start()

    @pl.when(south)
    def _():
        for copy in southward:
            copy.start()

    for copy in sideways:
        copy.start()

    get_cond.wait()

    def eliminate(k, carry):
        ratio, value, above, source, coupling = carry
        spread_out = spacing[k] + coupling + above * (1.0 - ratio)
        inverse = 1.0 / spread_out
        ratio = coupling * inverse
        value = (source + above * value) * inverse
        ratios[k] = ratio
        values[k] = value
        return ratio, value

    def forward(step, carry):
        ratio, value, above = carry
        for j in range(GROUP):
            k = step * GROUP + j
            coupling = jnp.where(k + 1 < wet, cond[k].astype(jnp.float32), 0.0)
            source = spacing[k] * heat[k].astype(jnp.float32)
            ratio, value = eliminate(k, (ratio, value, above, source, coupling))
            above = coupling
        return ratio, value, above

    zero = jnp.zeros((rows, cols), jnp.float32)
    whole = (levels - 1) // GROUP
    ratio, value, above = lax.fori_loop(0, whole, forward, (zero, zero, zero))
    for k in range(whole * GROUP, levels):
        source = spacing[k] * heat[k].astype(jnp.float32)
        if k < levels - 1:
            coupling = jnp.where(k + 1 < wet, cond[k].astype(jnp.float32), 0.0)
        else:
            coupling = zero
        ratio, value = eliminate(k, (ratio, value, above, source, coupling))
        above = coupling

    @pl.when(south)
    def _():
        for copy in northward:
            copy.wait_recv()

    @pl.when(north)
    def _():
        for copy in southward:
            copy.wait_recv()

    for copy in sideways:
        copy.wait_recv()

    from_n, from_s = land_n[...], land_s[...]
    ext[0, rows:, :cols] = jnp.where(sub8 < 4, from_s[:8], from_n[:8])
    ext[1, rows:, :cols] = pltpu.roll(jnp.where(sub8 >= 4, from_s[:8], from_n[:8]), 4, 0)
    ext[2, rows:, :cols] = jnp.where(sub8 < 4, from_s[8:], from_n[8:])
    sub_c = lax.broadcasted_iota(jnp.int32, (8, 128), 0)
    east_side = jnp.concatenate([land_e[...], jnp.where(sub_c < 4, land_c[3], land_c[1])], axis=0)
    west_side = jnp.concatenate([land_w[...], jnp.where(sub_c < 4, land_c[2], land_c[0])], axis=0)
    lane_x = lax.broadcasted_iota(jnp.int32, (rows + 8, 128), 1)
    for slot in range(3):
        ext[slot, :, cols:] = jnp.where(
            lane_x < 64, shift(east_side, -SLOT * slot), shift(west_side, SLOT * slot)
        )

    e, m = ext[0], ext[1]
    half_e, half_m = 0.5 * e, 0.5 * m
    centre = SURFACE + (half_e * spread(m) + half_m * spread(e))
    bound = 2.0 * centre[:rows, :cols] - SURFACE
    bound = jnp.max(bound, axis=0, keepdims=True)
    local = bound[:, :128]
    for start in range(128, cols, 128):
        local = jnp.maximum(local, bound[:, start : start + 128])
    col_max[0] = local

    def tell(buffer, off, sends, recvs, target):
        return pltpu.make_async_remote_copy(
            src_ref=buffer.at[0],
            dst_ref=buffer.at[off],
            send_sem=sends.at[off],
            recv_sem=recvs.at[off],
            device_id=target,
            device_id_type=MESH,
        )

    col_tells = [
        tell(col_max, off, col_send, col_recv, (row, lax.rem(col + off, n_col)))
        for off in range(1, n_col)
    ]
    row_tells = [
        tell(row_max, off, row_send, row_recv, (lax.rem(row + off, n_row), col))
        for off in range(1, n_row)
    ]
    for copy in col_tells:
        copy.start()

    parts = out_sem.shape[0] - 1
    per = levels // parts

    def backward_part(part, carry):
        def backward(step, carry):
            for j in range(GROUP):
                k = (part + 1) * per - 1 - (step * GROUP + j)
                carry = values[k] + ratios[k] * carry
                values[k] = carry
            return carry

        carry = lax.fori_loop(0, per // GROUP, backward, carry)
        span = pl.ds(part * per, per)
        put = pltpu.make_async_copy(values.at[span], out_hbm.at[span], out_sem.at[part])
        put.start()
        return carry, put

    carry = zero
    puts = []
    for part in reversed(range(parts // 2, parts)):
        carry, put = backward_part(part, carry)
        puts.append(put)

    for copy in col_tells:
        copy.wait_recv()
    best = col_max[0]
    for off in range(1, n_col):
        best = jnp.maximum(best, col_max[off])
    row_max[0] = best
    for copy in row_tells:
        copy.start()

    for part in reversed(range(parts // 2)):
        carry, put = backward_part(part, carry)
        puts.append(put)

    for copy in row_tells:
        copy.wait_recv()
    best = row_max[0]
    for off in range(1, n_row):
        best = jnp.maximum(best, row_max[off])
    top = jnp.max(best, axis=1, keepdims=True)

    theta = 0.5 * (top + SURFACE)
    delta = 0.5 * (top - SURFACE)
    sigma = theta / delta
    residual = ext[2]
    direction = residual * (1.0 / theta)
    recur = 1.0 / sigma
    result = jnp.zeros_like(residual)
    for _ in range(ITERS):
        result = result + direction
        image = centre * direction - (
            half_e * spread(m * direction) + half_m * spread(e * direction)
        )
        residual = residual - image
        recur_next = 1.0 / (2.0 * sigma - recur)
        direction = (recur_next * recur) * direction + (2.0 * recur_next / delta) * residual
        recur = recur_next
    height_ref[...] = (result + direction)[:rows, :cols]
    put = pltpu.make_async_copy(height_ref, height_hbm, out_sem.at[parts])
    put.start()
    puts.append(put)

    @pl.when(north)
    def _():
        for copy in northward:
            copy.wait_send()

    @pl.when(south)
    def _():
        for copy in southward:
            copy.wait_send()

    for copy in sideways + tuple(col_tells) + tuple(row_tells):
        copy.wait_send()
    for put in puts:
        put.wait()


def store(heat, height, heat_out, height_out, sem):
    parts = sem.shape[0] - 1
    per = heat.shape[0] // parts
    puts = [pltpu.make_async_copy(height, height_out, sem.at[parts])]
    for part in range(parts):
        span = pl.ds(part * per, per)
        puts.append(pltpu.make_async_copy(heat.at[span], heat_out.at[span], sem.at[part]))
    for put in puts:
        put.start()
    for put in puts:
        put.wait()


def local(n_row, n_col, heat, cond, spacing, wet, water, depth):
    levels, rows, cols = heat.shape
    f32 = jnp.float32
    hbm = pl.BlockSpec(memory_space=pltpu.HBM)
    dma = pltpu.SemaphoreType.DMA
    shapes = (
        jax.ShapeDtypeStruct((levels, rows, cols), f32),
        jax.ShapeDtypeStruct((rows, cols), f32),
    )
    mixed, height = pl.pallas_call(
        functools.partial(kernel, n_row, n_col),
        out_shape=shapes,
        in_specs=[hbm] * 6,
        out_specs=(hbm, hbm),
        scratch_shapes=[
            pltpu.VMEM((levels, rows, cols), heat.dtype),
            pltpu.VMEM((levels - 1, rows, cols), cond.dtype),
            pltpu.SMEM((levels,), f32),
            pltpu.VMEM((rows, cols), wet.dtype),
            pltpu.VMEM((rows, cols), water.dtype),
            pltpu.VMEM((rows, cols), f32),
            pltpu.VMEM((levels, rows, cols), f32),
            pltpu.VMEM((levels, rows, cols), f32),
            pltpu.VMEM((rows, cols), f32),
            pltpu.VMEM((3, rows + 8, cols + 128), f32),
            pltpu.VMEM((16, cols), f32),
            pltpu.VMEM((16, cols), f32),
            pltpu.VMEM((rows, 128), f32),
            pltpu.VMEM((rows, 128), f32),
            pltpu.VMEM((16, cols), f32),
            pltpu.VMEM((16, cols), f32),
            pltpu.VMEM((rows, 128), f32),
            pltpu.VMEM((rows, 128), f32),
            pltpu.VMEM((4, 8, 128), f32),
            pltpu.VMEM((n_col, 1, 128), f32),
            pltpu.VMEM((n_row, 1, 128), f32),
            dma((6,)),
            dma((5,)),
            dma((8,)),
            dma((8,)),
            dma((n_col,)),
            dma((n_col,)),
            dma((n_row,)),
            dma((n_row,)),
        ],
        compiler_params=pltpu.CompilerParams(
            collective_id=0, has_side_effects=True, vmem_limit_bytes=GRANT
        ),
    )(heat, cond, spacing, wet, water, depth)
    return pl.pallas_call(
        store,
        out_shape=shapes,
        in_specs=[hbm, hbm],
        out_specs=(hbm, hbm),
        scratch_shapes=[dma((5,))],
        compiler_params=pltpu.CompilerParams(has_side_effects=True, vmem_limit_bytes=GRANT),
    )(mixed, height)


def solution(mesh):
    placed = (
        P(None, "row", "col"),
        P(None, "row", "col"),
        P(),
        P("row", "col"),
        P("row", "col"),
        P("row", "col"),
    )
    return jax.shard_map(
        functools.partial(local, mesh.shape["row"], mesh.shape["col"]),
        mesh=mesh,
        in_specs=placed,
        out_specs=(P(None, "row", "col"), P("row", "col")),
        check_vma=False,
    )
```

```python
import functools
import math

import jax
import jax.numpy as jnp
from jax import lax
from jax.experimental import pallas as pl
from jax.experimental.pallas import tpu as pltpu
from jax.sharding import PartitionSpec as P

ITERS = 4
SURFACE = 0.5
MESH = pl.DeviceIdType.MESH
GROUP = 4
GRANT = 32 * 1024 * 1024
SLOT = 8


def spread(field):
    rows, lanes = field.shape
    t = pltpu.roll(field, 1, 0) + pltpu.roll(field, rows - 1, 0)
    h = field + 0.5 * t
    return t + (pltpu.roll(h, 1, 1) + pltpu.roll(h, lanes - 1, 1))


def shift(block, by):
    lanes = block.shape[1]
    by = by % lanes
    return block if by == 0 else pltpu.roll(block, by, 1)


def kernel(
    n_row,
    n_col,
    heat_hbm,
    cond_hbm,
    spacing_hbm,
    wet_hbm,
    water_hbm,
    depth_hbm,
    values,
    height_ref,
    heat,
    cond,
    spacing,
    wet_ref,
    water_ref,
    depth_ref,
    ratios,
    ext,
    top_stage,
    bot_stage,
    west_stage,
    east_stage,
    land_n,
    land_s,
    land_w,
    land_e,
    land_c,
    col_max,
    row_max,
    in_sem,
    send_sem,
    recv_sem,
    col_send,
    col_recv,
    row_send,
    row_recv,
):
    levels, rows, cols = heat.shape
    half = cols - 128
    row, col = lax.axis_index("row"), lax.axis_index("col")
    north, south = row > 0, row < n_row - 1
    up, down = lax.rem(row + n_row - 1, n_row), lax.rem(row + 1, n_row)
    west, east = lax.rem(col + n_col - 1, n_col), lax.rem(col + 1, n_col)

    pairs = (
        (wet_hbm, wet_ref),
        (spacing_hbm, spacing),
        (water_hbm, water_ref),
        (depth_hbm, depth_ref),
        (heat_hbm, heat),
        (cond_hbm, cond),
    )
    gets = [pltpu.make_async_copy(a, b, in_sem.at[i]) for i, (a, b) in enumerate(pairs)]
    for get in gets:
        get.start()
    get_cond = gets.pop()

    barrier = pltpu.get_barrier_semaphore()

    def greet(r, c):
        pl.semaphore_signal(barrier, inc=1, device_id=(r, c), device_id_type=MESH)

    for off in range(1, n_col):
        greet(row, lax.rem(col + off, n_col))
    for off in range(1, n_row):
        greet(lax.rem(row + off, n_row), col)

    @pl.when(north)
    def _():
        greet(up, west)
        greet(up, east)

    @pl.when(south)
    def _():
        greet(down, west)
        greet(down, east)

    @pl.when(jnp.logical_not(north))
    def _():
        land_n[...] = jnp.zeros_like(land_n)
        land_c[0] = jnp.zeros_like(land_c[0])
        land_c[1] = jnp.zeros_like(land_c[1])

    @pl.when(jnp.logical_not(south))
    def _():
        land_s[...] = jnp.zeros_like(land_s)
        land_c[2] = jnp.zeros_like(land_c[2])
        land_c[3] = jnp.zeros_like(land_c[3])

    for get in gets:
        get.wait()
    wet = wet_ref[...]
    mask = water_ref[...].astype(jnp.float32)
    masked_depth = mask * depth_ref[...]

    def add_levels(step, total):
        for j in range(GROUP):
            k = step * GROUP + j
            total = total + jnp.where(k < wet, spacing[k] * heat[k].astype(jnp.float32), 0.0)
        return total

    total = lax.fori_loop(0, levels // GROUP, add_levels, jnp.zeros((rows, cols), jnp.float32))
    forcing = mask * total / math.sqrt(levels)

    fields = (masked_depth, mask, forcing)
    for slot, field in enumerate(fields):
        ext[slot, :rows, :cols] = field
    sub8 = lax.broadcasted_iota(jnp.int32, (8, cols), 0)
    top_stage[0:8] = jnp.where(sub8 < 4, masked_depth[:8], pltpu.roll(mask[:8], 4, 0))
    top_stage[8:16] = forcing[:8]
    bot_stage[0:8] = jnp.where(sub8 >= 4, masked_depth[rows - 8 :], pltpu.roll(mask[rows - 8 :], 4, 0))
    bot_stage[8:16] = forcing[rows - 8 :]
    lane = lax.broadcasted_iota(jnp.int32, (rows, 128), 1)
    west_stage[...] = jnp.where(
        lane < SLOT,
        masked_depth[:, :128],
        jnp.where(lane < 2 * SLOT, shift(mask[:, :128], SLOT), shift(forcing[:, :128], 2 * SLOT)),
    )
    east_stage[...] = jnp.where(
        lane >= 128 - SLOT,
        masked_depth[:, half:],
        jnp.where(
            lane >= 128 - 2 * SLOT, shift(mask[:, half:], -SLOT), shift(forcing[:, half:], -2 * SLOT)
        ),
    )

    def remote(src, dst, slot, target):
        return pltpu.make_async_remote_copy(
            src_ref=src,
            dst_ref=dst,
            send_sem=send_sem.at[slot],
            recv_sem=recv_sem.at[slot],
            device_id=target,
            device_id_type=MESH,
        )

    low, high = pl.ds(0, 8), pl.ds(rows - 8, 8)
    to_n = remote(top_stage, land_s, 0, (up, col))
    to_s = remote(bot_stage, land_n, 1, (down, col))
    to_w = remote(west_stage, land_e, 2, (row, west))
    to_e = remote(east_stage, land_w, 3, (row, east))
    to_nw = remote(west_stage.at[low], land_c.at[3], 4, (up, west))
    to_ne = remote(east_stage.at[low], land_c.at[2], 5, (up, east))
    to_sw = remote(west_stage.at[high], land_c.at[1], 6, (down, west))
    to_se = remote(east_stage.at[high], land_c.at[0], 7, (down, east))
    northward, southward, sideways = (to_n, to_nw, to_ne), (to_s, to_sw, to_se), (to_w, to_e)

    diagonal = 2 * (north.astype(jnp.int32) + south.astype(jnp.int32))
    pl.semaphore_wait(barrier, n_row + n_col - 2 + diagonal)

    @pl.when(north)
    def _():
        for copy in northward:
            copy.start()

    @pl.when(south)
    def _():
        for copy in southward:
            copy.start()

    for copy in sideways:
        copy.start()

    get_cond.wait()

    def eliminate(k, carry):
        ratio, value, above, source, coupling = carry
        spread_out = spacing[k] + coupling + above * (1.0 - ratio)
        inverse = 1.0 / spread_out
        ratio = coupling * inverse
        value = (source + above * value) * inverse
        ratios[k] = ratio
        values[k] = value
        return ratio, value

    def forward(step, carry):
        ratio, value, above = carry
        for j in range(GROUP):
            k = step * GROUP + j
            coupling = jnp.where(k + 1 < wet, cond[k].astype(jnp.float32), 0.0)
            source = spacing[k] * heat[k].astype(jnp.float32)
            ratio, value = eliminate(k, (ratio, value, above, source, coupling))
            above = coupling
        return ratio, value, above

    zero = jnp.zeros((rows, cols), jnp.float32)
    whole = (levels - 1) // GROUP
    ratio, value, above = lax.fori_loop(0, whole, forward, (zero, zero, zero))
    for k in range(whole * GROUP, levels):
        source = spacing[k] * heat[k].astype(jnp.float32)
        if k < levels - 1:
            coupling = jnp.where(k + 1 < wet, cond[k].astype(jnp.float32), 0.0)
        else:
            coupling = zero
        ratio, value = eliminate(k, (ratio, value, above, source, coupling))
        above = coupling

    @pl.when(south)
    def _():
        for copy in northward:
            copy.wait_recv()

    @pl.when(north)
    def _():
        for copy in southward:
            copy.wait_recv()

    for copy in sideways:
        copy.wait_recv()

    from_n, from_s = land_n[...], land_s[...]
    ext[0, rows:, :cols] = jnp.where(sub8 < 4, from_s[:8], from_n[:8])
    ext[1, rows:, :cols] = pltpu.roll(jnp.where(sub8 >= 4, from_s[:8], from_n[:8]), 4, 0)
    ext[2, rows:, :cols] = jnp.where(sub8 < 4, from_s[8:], from_n[8:])
    sub_c = lax.broadcasted_iota(jnp.int32, (8, 128), 0)
    east_side = jnp.concatenate([land_e[...], jnp.where(sub_c < 4, land_c[3], land_c[1])], axis=0)
    west_side = jnp.concatenate([land_w[...], jnp.where(sub_c < 4, land_c[2], land_c[0])], axis=0)
    lane_x = lax.broadcasted_iota(jnp.int32, (rows + 8, 128), 1)
    for slot in range(3):
        ext[slot, :, cols:] = jnp.where(
            lane_x < 64, shift(east_side, -SLOT * slot), shift(west_side, SLOT * slot)
        )

    e, m = ext[0], ext[1]
    half_e, half_m = 0.5 * e, 0.5 * m
    centre = SURFACE + (half_e * spread(m) + half_m * spread(e))
    bound = 2.0 * centre[:rows, :cols] - SURFACE
    bound = jnp.max(bound, axis=0, keepdims=True)
    local = bound[:, :128]
    for start in range(128, cols, 128):
        local = jnp.maximum(local, bound[:, start : start + 128])
    col_max[0] = local

    def tell(buffer, off, sends, recvs, target):
        return pltpu.make_async_remote_copy(
            src_ref=buffer.at[0],
            dst_ref=buffer.at[off],
            send_sem=sends.at[off],
            recv_sem=recvs.at[off],
            device_id=target,
            device_id_type=MESH,
        )

    col_tells = [
        tell(col_max, off, col_send, col_recv, (row, lax.rem(col + off, n_col)))
        for off in range(1, n_col)
    ]
    row_tells = [
        tell(row_max, off, row_send, row_recv, (lax.rem(row + off, n_row), col))
        for off in range(1, n_row)
    ]
    for copy in col_tells:
        copy.start()

    parts = 2
    per = levels // parts

    def backward_part(part, carry):
        def backward(step, carry):
            for j in range(GROUP):
                k = (part + 1) * per - 1 - (step * GROUP + j)
                carry = values[k] + ratios[k] * carry
                values[k] = carry
            return carry

        return lax.fori_loop(0, per // GROUP, backward, carry)

    carry = backward_part(1, zero)

    for copy in col_tells:
        copy.wait_recv()
    best = col_max[0]
    for off in range(1, n_col):
        best = jnp.maximum(best, col_max[off])
    row_max[0] = best
    for copy in row_tells:
        copy.start()

    backward_part(0, carry)

    for copy in row_tells:
        copy.wait_recv()
    best = row_max[0]
    for off in range(1, n_row):
        best = jnp.maximum(best, row_max[off])
    top = jnp.max(best, axis=1, keepdims=True)

    theta = 0.5 * (top + SURFACE)
    delta = 0.5 * (top - SURFACE)
    sigma = theta / delta
    residual = ext[2]
    direction = residual * (1.0 / theta)
    recur = 1.0 / sigma
    result = jnp.zeros_like(residual)
    for _ in range(ITERS):
        result = result + direction
        image = centre * direction - (
            half_e * spread(m * direction) + half_m * spread(e * direction)
        )
        residual = residual - image
        recur_next = 1.0 / (2.0 * sigma - recur)
        direction = (recur_next * recur) * direction + (2.0 * recur_next / delta) * residual
        recur = recur_next
    height_ref[...] = (result + direction)[:rows, :cols]

    @pl.when(north)
    def _():
        for copy in northward:
            copy.wait_send()

    @pl.when(south)
    def _():
        for copy in southward:
            copy.wait_send()

    for copy in sideways + tuple(col_tells) + tuple(row_tells):
        copy.wait_send()


def store(heat, height, heat_out, height_out, sem):
    parts = sem.shape[0] - 1
    per = heat.shape[0] // parts
    puts = [pltpu.make_async_copy(height, height_out, sem.at[parts])]
    for part in range(parts):
        span = pl.ds(part * per, per)
        puts.append(pltpu.make_async_copy(heat.at[span], heat_out.at[span], sem.at[part]))
    for put in puts:
        put.start()
    for put in puts:
        put.wait()


def local(n_row, n_col, heat, cond, spacing, wet, water, depth):
    levels, rows, cols = heat.shape
    f32 = jnp.float32
    vmem = pl.BlockSpec(memory_space=pltpu.VMEM)
    hbm = pl.BlockSpec(memory_space=pltpu.HBM)
    dma = pltpu.SemaphoreType.DMA
    shapes = (
        jax.ShapeDtypeStruct((levels, rows, cols), f32),
        jax.ShapeDtypeStruct((rows, cols), f32),
    )
    held = [
        pltpu.with_memory_space_constraint(x, pltpu.HBM)
        for x in (heat, cond, spacing, wet, water, depth)
    ]
    mixed, height = pl.pallas_call(
        functools.partial(kernel, n_row, n_col),
        out_shape=shapes,
        in_specs=[hbm] * 6,
        out_specs=(vmem, vmem),
        scratch_shapes=[
            pltpu.VMEM((levels, rows, cols), heat.dtype),
            pltpu.VMEM((levels - 1, rows, cols), cond.dtype),
            pltpu.SMEM((levels,), f32),
            pltpu.VMEM((rows, cols), wet.dtype),
            pltpu.VMEM((rows, cols), water.dtype),
            pltpu.VMEM((rows, cols), f32),
            pltpu.VMEM((levels, rows, cols), f32),
            pltpu.VMEM((3, rows + 8, cols + 128), f32),
            pltpu.VMEM((16, cols), f32),
            pltpu.VMEM((16, cols), f32),
            pltpu.VMEM((rows, 128), f32),
            pltpu.VMEM((rows, 128), f32),
            pltpu.VMEM((16, cols), f32),
            pltpu.VMEM((16, cols), f32),
            pltpu.VMEM((rows, 128), f32),
            pltpu.VMEM((rows, 128), f32),
            pltpu.VMEM((4, 8, 128), f32),
            pltpu.VMEM((n_col, 1, 128), f32),
            pltpu.VMEM((n_row, 1, 128), f32),
            dma((6,)),
            dma((8,)),
            dma((8,)),
            dma((n_col,)),
            dma((n_col,)),
            dma((n_row,)),
            dma((n_row,)),
        ],
        compiler_params=pltpu.CompilerParams(
            collective_id=0, has_side_effects=True, vmem_limit_bytes=GRANT
        ),
    )(*held)
    return pl.pallas_call(
        store,
        out_shape=shapes,
        in_specs=[vmem, vmem],
        out_specs=(hbm, hbm),
        scratch_shapes=[dma((5,))],
        compiler_params=pltpu.CompilerParams(has_side_effects=True, vmem_limit_bytes=GRANT),
    )(mixed, height)


def solution(mesh):
    placed = (
        P(None, "row", "col"),
        P(None, "row", "col"),
        P(),
        P("row", "col"),
        P("row", "col"),
        P("row", "col"),
    )
    return jax.shard_map(
        functools.partial(local, mesh.shape["row"], mesh.shape["col"]),
        mesh=mesh,
        in_specs=placed,
        out_specs=(P(None, "row", "col"), P("row", "col")),
        check_vma=False,
    )
```

```python
import functools
import math

import jax
import jax.numpy as jnp
from jax import lax
from jax.experimental import pallas as pl
from jax.experimental.pallas import tpu as pltpu
from jax.sharding import PartitionSpec as P

ITERS = 4
SURFACE = 0.5
MESH = pl.DeviceIdType.MESH
GROUP = 4
GRANT = 32 * 1024 * 1024
SLOT = 8


def spread(field):
    rows, lanes = field.shape
    t = pltpu.roll(field, 1, 0) + pltpu.roll(field, rows - 1, 0)
    h = field + 0.5 * t
    return t + (pltpu.roll(h, 1, 1) + pltpu.roll(h, lanes - 1, 1))


def shift(block, by):
    lanes = block.shape[1]
    by = by % lanes
    return block if by == 0 else pltpu.roll(block, by, 1)


def pack_west(blocks):
    lane = lax.broadcasted_iota(jnp.int32, blocks[0].shape, 1)
    out = blocks[0]
    for slot in range(1, len(blocks)):
        out = jnp.where(lane >= SLOT * slot, shift(blocks[slot], SLOT * slot), out)
    return out


def pack_east(blocks):
    lane = lax.broadcasted_iota(jnp.int32, blocks[0].shape, 1)
    out = blocks[0]
    for slot in range(1, len(blocks)):
        out = jnp.where(lane < 128 - SLOT * slot, shift(blocks[slot], -SLOT * slot), out)
    return out


def kernel(
    n_row,
    n_col,
    heat_hbm,
    cond_hbm,
    spacing_hbm,
    wet_hbm,
    water_hbm,
    depth_hbm,
    ratios,
    values,
    height_ref,
    heat,
    cond,
    spacing,
    wet_ref,
    water_ref,
    depth_ref,
    ext,
    edge,
    side,
    land_edge,
    land_side,
    col_max,
    row_max,
    in_sem,
    send_sem,
    recv_sem,
    col_send,
    col_recv,
    row_send,
    row_recv,
):
    levels, rows, cols = heat.shape
    half = cols - 128
    tiles = rows // 8
    row, col = lax.axis_index("row"), lax.axis_index("col")
    north, south = row > 0, row < n_row - 1
    up, down = lax.rem(row + n_row - 1, n_row), lax.rem(row + 1, n_row)
    west, east = lax.rem(col + n_col - 1, n_col), lax.rem(col + 1, n_col)

    pairs = (
        (water_hbm, water_ref),
        (depth_hbm, depth_ref),
        (wet_hbm, wet_ref),
        (spacing_hbm, spacing),
        (heat_hbm, heat),
        (cond_hbm, cond),
    )
    gets = [pltpu.make_async_copy(a, b, in_sem.at[i]) for i, (a, b) in enumerate(pairs)]
    for get in gets:
        get.start()

    barrier = pltpu.get_barrier_semaphore()

    def greet(r, c):
        pl.semaphore_signal(barrier, inc=1, device_id=(r, c), device_id_type=MESH)

    for off in range(1, n_col):
        greet(row, lax.rem(col + off, n_col))
    for off in range(1, n_row):
        greet(lax.rem(row + off, n_row), col)

    @pl.when(north)
    def _():
        greet(up, west)
        greet(up, east)

    @pl.when(south)
    def _():
        greet(down, west)
        greet(down, east)

    @pl.when(jnp.logical_not(north))
    def _():
        for kind in range(2):
            for place in (2, 3):
                land_side[kind, place] = jnp.zeros((8, 128), jnp.float32)
            land_edge[kind, 0] = jnp.zeros((8, cols), jnp.float32)

    @pl.when(jnp.logical_not(south))
    def _():
        for kind in range(2):
            for place in (4, 5):
                land_side[kind, place] = jnp.zeros((8, 128), jnp.float32)
            land_edge[kind, 1] = jnp.zeros((8, cols), jnp.float32)

    def halo_copies(kind):
        def remote(src, dst, slot, target):
            return pltpu.make_async_remote_copy(
                src_ref=src,
                dst_ref=dst,
                send_sem=send_sem.at[kind, slot],
                recv_sem=recv_sem.at[kind, slot],
                device_id=target,
                device_id_type=MESH,
            )

        from_west, from_east = side.at[kind, 0], side.at[kind, 1]
        northward = (
            remote(edge.at[kind, 0], land_edge.at[kind, 1], 0, (up, col)),
            remote(from_west, land_side.at[kind, 5], 1, (up, west)),
            remote(from_east, land_side.at[kind, 4], 2, (up, east)),
        )
        southward = (
            remote(edge.at[kind, 1], land_edge.at[kind, 0], 3, (down, col)),
            remote(from_west, land_side.at[kind, 3], 4, (down, west)),
            remote(from_east, land_side.at[kind, 2], 5, (down, east)),
        )
        sideways = (
            remote(from_west, land_side.at[kind, 1], 6, (row, west)),
            remote(from_east, land_side.at[kind, 0], 7, (row, east)),
        )
        return northward, southward, sideways

    def start_halo(kind):
        northward, southward, sideways = halo_copies(kind)

        @pl.when(north)
        def _():
            for copy in northward:
                copy.start()

        @pl.when(south)
        def _():
            for copy in southward:
                copy.start()

        for copy in sideways:
            copy.start()

    def wait_halo(kind):
        northward, southward, sideways = halo_copies(kind)

        @pl.when(south)
        def _():
            for copy in northward:
                copy.wait_recv()

        @pl.when(north)
        def _():
            for copy in southward:
                copy.wait_recv()

        for copy in sideways:
            copy.wait_recv()

    def end_halo(kind):
        northward, southward, sideways = halo_copies(kind)

        @pl.when(north)
        def _():
            for copy in northward:
                copy.wait_send()

        @pl.when(south)
        def _():
            for copy in southward:
                copy.wait_send()

        for copy in sideways:
            copy.wait_send()

    def stage_sides(kind, fields):
        blocks = [f[8 * t : 8 * t + 8, :128] for f in fields for t in range(tiles)]
        side[kind, 0] = pack_west(blocks)
        blocks = [f[8 * t : 8 * t + 8, half:] for f in fields for t in range(tiles)]
        side[kind, 1] = pack_east(blocks)

    sub_c = lax.broadcasted_iota(jnp.int32, (8, 128), 0)
    lane_c = lax.broadcasted_iota(jnp.int32, (8, 128), 1)

    def widen_sides(kind, slot, target):
        w, e, nw, ne, sw, se = (land_side[kind, place] for place in range(6))
        for t in range(tiles):
            by = SLOT * (slot * tiles + t)
            ext[target, pl.ds(8 * t, 8), cols:] = jnp.where(lane_c < 64, shift(e, -by), shift(w, by))
        first, last = SLOT * slot * tiles, SLOT * (slot * tiles + tiles - 1)
        above = jnp.where(lane_c < 64, shift(ne, -last), shift(nw, last))
        below = jnp.where(lane_c < 64, shift(se, -first), shift(sw, first))
        ext[target, rows:, cols:] = jnp.where(sub_c < 4, below, above)

    gets[0].wait()
    gets[1].wait()
    mask = water_ref[...].astype(jnp.float32)
    masked_depth = mask * depth_ref[...]
    ext[0, :rows, :cols] = masked_depth
    ext[1, :rows, :cols] = mask
    sub8 = lax.broadcasted_iota(jnp.int32, (8, cols), 0)
    edge[0, 0] = jnp.where(sub8 < 4, masked_depth[:8], pltpu.roll(mask[:8], 4, 0))
    edge[0, 1] = jnp.where(sub8 >= 4, masked_depth[rows - 8 :], pltpu.roll(mask[rows - 8 :], 4, 0))
    stage_sides(0, (masked_depth, mask))

    diagonal = 2 * (north.astype(jnp.int32) + south.astype(jnp.int32))
    pl.semaphore_wait(barrier, n_row + n_col - 2 + diagonal)
    start_halo(0)

    for get in gets[2:5]:
        get.wait()
    wet = wet_ref[...]

    def add_levels(step, total):
        for j in range(GROUP):
            k = step * GROUP + j
            total = total + jnp.where(k < wet, spacing[k] * heat[k].astype(jnp.float32), 0.0)
        return total

    zero = jnp.zeros((rows, cols), jnp.float32)
    total = lax.fori_loop(0, levels // GROUP, add_levels, zero)
    forcing = mask * total / math.sqrt(levels)
    ext[2, :rows, :cols] = forcing
    edge[1, 0] = forcing[:8]
    edge[1, 1] = forcing[rows - 8 :]
    stage_sides(1, (forcing,))
    start_halo(1)

    wait_halo(0)
    from_n, from_s = land_edge[0, 0], land_edge[0, 1]
    ext[0, rows:, :cols] = jnp.where(sub8 < 4, from_s, from_n)
    ext[1, rows:, :cols] = pltpu.roll(jnp.where(sub8 >= 4, from_s, from_n), 4, 0)
    widen_sides(0, 0, 0)
    widen_sides(0, 1, 1)
    e, m = ext[0], ext[1]
    half_e, half_m = 0.5 * e, 0.5 * m
    centre = SURFACE + (half_e * spread(m) + half_m * spread(e))
    ext[3] = centre
    bound = jnp.max(2.0 * centre[:rows, :cols] - SURFACE, axis=0, keepdims=True)
    local = bound[:, :128]
    for start in range(128, cols, 128):
        local = jnp.maximum(local, bound[:, start : start + 128])
    col_max[0] = local

    def tell(buffer, off, sends, recvs, target):
        return pltpu.make_async_remote_copy(
            src_ref=buffer.at[0],
            dst_ref=buffer.at[off],
            send_sem=sends.at[off],
            recv_sem=recvs.at[off],
            device_id=target,
            device_id_type=MESH,
        )

    col_tells = [
        tell(col_max, off, col_send, col_recv, (row, lax.rem(col + off, n_col)))
        for off in range(1, n_col)
    ]
    row_tells = [
        tell(row_max, off, row_send, row_recv, (lax.rem(row + off, n_row), col))
        for off in range(1, n_row)
    ]
    for copy in col_tells:
        copy.start()

    gets[5].wait()

    def eliminate(k, carry, coupling):
        ratio, value, above = carry
        inverse = 1.0 / (spacing[k] + coupling + above * (1.0 - ratio))
        source = spacing[k] * heat[k].astype(jnp.float32)
        ratio = coupling * inverse
        value = (source + above * value) * inverse
        ratios[k] = ratio
        values[k] = value
        return ratio, value, coupling

    def forward(step, carry):
        for j in range(GROUP):
            k = step * GROUP + j
            coupling = jnp.where(k + 1 < wet_ref[...], cond[k].astype(jnp.float32), 0.0)
            carry = eliminate(k, carry, coupling)
        return carry

    steps = (levels - 1) // GROUP
    carry = lax.fori_loop(0, steps // 2, forward, (zero, zero, zero))

    for copy in col_tells:
        copy.wait_recv()
    best = col_max[0]
    for off in range(1, n_col):
        best = jnp.maximum(best, col_max[off])
    row_max[0] = best
    for copy in row_tells:
        copy.start()

    carry = lax.fori_loop(steps // 2, steps, forward, carry)
    for k in range(steps * GROUP, levels):
        coupling = zero
        if k < levels - 1:
            coupling = jnp.where(k + 1 < wet_ref[...], cond[k].astype(jnp.float32), 0.0)
        carry = eliminate(k, carry, coupling)

    wait_halo(1)
    ext[2, rows:, :cols] = jnp.where(sub8 < 4, land_edge[1, 1], land_edge[1, 0])
    widen_sides(1, 0, 2)

    for copy in row_tells:
        copy.wait_recv()
    best = row_max[0]
    for off in range(1, n_row):
        best = jnp.maximum(best, row_max[off])
    top = jnp.max(best, axis=1, keepdims=True)

    theta = 0.5 * (top + SURFACE)
    delta = 0.5 * (top - SURFACE)
    sigma = theta / delta
    e, m, residual, centre = ext[0], ext[1], ext[2], ext[3]
    half_e, half_m = 0.5 * e, 0.5 * m
    direction = residual * (1.0 / theta)
    recur = 1.0 / sigma
    result = jnp.zeros_like(residual)
    for _ in range(ITERS):
        result = result + direction
        image = centre * direction - (
            half_e * spread(m * direction) + half_m * spread(e * direction)
        )
        residual = residual - image
        recur_next = 1.0 / (2.0 * sigma - recur)
        direction = (recur_next * recur) * direction + (2.0 * recur_next / delta) * residual
        recur = recur_next
    height_ref[...] = (result + direction)[:rows, :cols]

    end_halo(0)
    end_halo(1)
    for copy in col_tells + row_tells:
        copy.wait_send()


def finish(ratios, values, height, heat_out, height_out, heat, sem):
    levels, rows, cols = values.shape
    parts = sem.shape[0] - 1
    per = levels // parts
    puts = [pltpu.make_async_copy(height, height_out, sem.at[parts])]
    puts[0].start()
    carry = jnp.zeros((rows, cols), jnp.float32)
    for part in reversed(range(parts)):
        for k in reversed(range(part * per, (part + 1) * per)):
            carry = values[k] + ratios[k] * carry
            heat[k] = carry
        span = pl.ds(part * per, per)
        puts.append(pltpu.make_async_copy(heat.at[span], heat_out.at[span], sem.at[part]))
        puts[-1].start()
    for put in puts:
        put.wait()


def local(n_row, n_col, heat, cond, spacing, wet, water, depth):
    levels, rows, cols = heat.shape
    f32 = jnp.float32
    parts = 6
    vmem = pl.BlockSpec(memory_space=pltpu.VMEM)
    hbm = pl.BlockSpec(memory_space=pltpu.HBM)
    dma = pltpu.SemaphoreType.DMA
    column = jax.ShapeDtypeStruct((levels, rows, cols), f32)
    surface = jax.ShapeDtypeStruct((rows, cols), f32)
    held = [
        pltpu.with_memory_space_constraint(x, pltpu.HBM)
        for x in (heat, cond, spacing, wet, water, depth)
    ]
    ratios, values, height = pl.pallas_call(
        functools.partial(kernel, n_row, n_col),
        out_shape=(column, column, surface),
        in_specs=[hbm] * 6,
        out_specs=(vmem, vmem, vmem),
        scratch_shapes=[
            pltpu.VMEM((levels, rows, cols), heat.dtype),
            pltpu.VMEM((levels - 1, rows, cols), cond.dtype),
            pltpu.SMEM((levels,), f32),
            pltpu.VMEM((rows, cols), wet.dtype),
            pltpu.VMEM((rows, cols), water.dtype),
            pltpu.VMEM((rows, cols), f32),
            pltpu.VMEM((4, rows + 8, cols + 128), f32),
            pltpu.VMEM((2, 2, 8, cols), f32),
            pltpu.VMEM((2, 2, 8, 128), f32),
            pltpu.VMEM((2, 2, 8, cols), f32),
            pltpu.VMEM((2, 6, 8, 128), f32),
            pltpu.VMEM((n_col, 1, 128), f32),
            pltpu.VMEM((n_row, 1, 128), f32),
            dma((6,)),
            dma((2, 8)),
            dma((2, 8)),
            dma((n_col,)),
            dma((n_col,)),
            dma((n_row,)),
            dma((n_row,)),
        ],
        compiler_params=pltpu.CompilerParams(
            collective_id=0, has_side_effects=True, vmem_limit_bytes=GRANT
        ),
    )(*held)
    return pl.pallas_call(
        finish,
        out_shape=(column, surface),
        in_specs=[vmem, vmem, vmem],
        out_specs=(hbm, hbm),
        scratch_shapes=[pltpu.VMEM((levels, rows, cols), f32), dma((parts + 1,))],
        compiler_params=pltpu.CompilerParams(has_side_effects=True, vmem_limit_bytes=GRANT),
    )(ratios, values, height)


def solution(mesh):
    placed = (
        P(None, "row", "col"),
        P(None, "row", "col"),
        P(),
        P("row", "col"),
        P("row", "col"),
        P("row", "col"),
    )
    return jax.shard_map(
        functools.partial(local, mesh.shape["row"], mesh.shape["col"]),
        mesh=mesh,
        in_specs=placed,
        out_specs=(P(None, "row", "col"), P("row", "col")),
        check_vma=False,
    )
```

```python
import functools
import math

import jax
import jax.numpy as jnp
from jax import lax
from jax.experimental import pallas as pl
from jax.experimental.pallas import tpu as pltpu
from jax.sharding import PartitionSpec as P

ITERS = 4
SURFACE = 0.5
MESH = pl.DeviceIdType.MESH
GROUP = 4
GRANT = 32 * 1024 * 1024
SLOT = 8


def spread(field):
    rows, lanes = field.shape
    t = pltpu.roll(field, 1, 0) + pltpu.roll(field, rows - 1, 0)
    h = field + 0.5 * t
    return t + (pltpu.roll(h, 1, 1) + pltpu.roll(h, lanes - 1, 1))


def shift(block, by):
    lanes = block.shape[1]
    by = by % lanes
    return block if by == 0 else pltpu.roll(block, by, 1)


def pack_west(blocks):
    lane = lax.broadcasted_iota(jnp.int32, blocks[0].shape, 1)
    out = blocks[0]
    for slot in range(1, len(blocks)):
        out = jnp.where(lane >= SLOT * slot, shift(blocks[slot], SLOT * slot), out)
    return out


def pack_east(blocks):
    lane = lax.broadcasted_iota(jnp.int32, blocks[0].shape, 1)
    out = blocks[0]
    for slot in range(1, len(blocks)):
        out = jnp.where(lane < 128 - SLOT * slot, shift(blocks[slot], -SLOT * slot), out)
    return out


def kernel(
    n_row,
    n_col,
    heat_hbm,
    cond_hbm,
    spacing_hbm,
    wet_hbm,
    water_hbm,
    depth_hbm,
    ratios,
    values,
    height_ref,
    heat,
    cond,
    spacing,
    wet_ref,
    water_ref,
    depth_ref,
    ext,
    edge,
    side,
    land_edge,
    land_side,
    maxima,
    in_sem,
    send_sem,
    recv_sem,
    max_send,
    max_recv,
):
    levels, rows, cols = heat.shape
    half = cols - 128
    tiles = rows // 8
    row, col = lax.axis_index("row"), lax.axis_index("col")
    north, south = row > 0, row < n_row - 1
    up, down = lax.rem(row + n_row - 1, n_row), lax.rem(row + 1, n_row)
    west, east = lax.rem(col + n_col - 1, n_col), lax.rem(col + 1, n_col)

    pairs = (
        (water_hbm, water_ref),
        (depth_hbm, depth_ref),
        (wet_hbm, wet_ref),
        (spacing_hbm, spacing),
        (heat_hbm, heat),
        (cond_hbm, cond),
    )
    gets = [pltpu.make_async_copy(a, b, in_sem.at[i]) for i, (a, b) in enumerate(pairs)]
    for get in gets:
        get.start()

    barrier = pltpu.get_barrier_semaphore()

    def greet(r, c):
        pl.semaphore_signal(barrier, inc=1, device_id=(r, c), device_id_type=MESH)

    def peer(i):
        return lax.rem(row + i // n_col, n_row), lax.rem(col + lax.rem(i, n_col), n_col)

    peers = n_row * n_col

    def for_peers(act):
        if peers <= 64:
            for i in range(1, peers):
                act(jnp.int32(i))
        else:
            lax.fori_loop(1, peers, lambda i, none: (act(i), none)[1], None)

    for_peers(lambda i: greet(*peer(i)))

    @pl.when(jnp.logical_not(north))
    def _():
        for kind in range(2):
            for place in (2, 3):
                land_side[kind, place] = jnp.zeros((8, 128), jnp.float32)
            land_edge[kind, 0] = jnp.zeros((8, cols), jnp.float32)

    @pl.when(jnp.logical_not(south))
    def _():
        for kind in range(2):
            for place in (4, 5):
                land_side[kind, place] = jnp.zeros((8, 128), jnp.float32)
            land_edge[kind, 1] = jnp.zeros((8, cols), jnp.float32)

    def halo_copies(kind):
        def remote(src, dst, slot, target):
            return pltpu.make_async_remote_copy(
                src_ref=src,
                dst_ref=dst,
                send_sem=send_sem.at[kind, slot],
                recv_sem=recv_sem.at[kind, slot],
                device_id=target,
                device_id_type=MESH,
            )

        from_west, from_east = side.at[kind, 0], side.at[kind, 1]
        northward = (
            remote(edge.at[kind, 0], land_edge.at[kind, 1], 0, (up, col)),
            remote(from_west, land_side.at[kind, 5], 1, (up, west)),
            remote(from_east, land_side.at[kind, 4], 2, (up, east)),
        )
        southward = (
            remote(edge.at[kind, 1], land_edge.at[kind, 0], 3, (down, col)),
            remote(from_west, land_side.at[kind, 3], 4, (down, west)),
            remote(from_east, land_side.at[kind, 2], 5, (down, east)),
        )
        sideways = (
            remote(from_west, land_side.at[kind, 1], 6, (row, west)),
            remote(from_east, land_side.at[kind, 0], 7, (row, east)),
        )
        return northward, southward, sideways

    def start_halo(kind):
        northward, southward, sideways = halo_copies(kind)

        @pl.when(north)
        def _():
            for copy in northward:
                copy.start()

        @pl.when(south)
        def _():
            for copy in southward:
                copy.start()

        for copy in sideways:
            copy.start()

    def wait_halo(kind):
        northward, southward, sideways = halo_copies(kind)

        @pl.when(south)
        def _():
            for copy in northward:
                copy.wait_recv()

        @pl.when(north)
        def _():
            for copy in southward:
                copy.wait_recv()

        for copy in sideways:
            copy.wait_recv()

    def end_halo(kind):
        northward, southward, sideways = halo_copies(kind)

        @pl.when(north)
        def _():
            for copy in northward:
                copy.wait_send()

        @pl.when(south)
        def _():
            for copy in southward:
                copy.wait_send()

        for copy in sideways:
            copy.wait_send()

    def stage_sides(kind, fields):
        blocks = [f[8 * t : 8 * t + 8, :128] for f in fields for t in range(tiles)]
        side[kind, 0] = pack_west(blocks)
        blocks = [f[8 * t : 8 * t + 8, half:] for f in fields for t in range(tiles)]
        side[kind, 1] = pack_east(blocks)

    sub_c = lax.broadcasted_iota(jnp.int32, (8, 128), 0)
    lane_c = lax.broadcasted_iota(jnp.int32, (8, 128), 1)

    def widen_sides(kind, slot, target):
        w, e, nw, ne, sw, se = (land_side[kind, place] for place in range(6))
        for t in range(tiles):
            by = SLOT * (slot * tiles + t)
            ext[target, pl.ds(8 * t, 8), cols:] = jnp.where(lane_c < 64, shift(e, -by), shift(w, by))
        first, last = SLOT * slot * tiles, SLOT * (slot * tiles + tiles - 1)
        above = jnp.where(lane_c < 64, shift(ne, -last), shift(nw, last))
        below = jnp.where(lane_c < 64, shift(se, -first), shift(sw, first))
        ext[target, rows:, cols:] = jnp.where(sub_c < 4, below, above)

    gets[0].wait()
    gets[1].wait()
    mask = water_ref[...].astype(jnp.float32)
    masked_depth = mask * depth_ref[...]
    ext[0, :rows, :cols] = masked_depth
    ext[1, :rows, :cols] = mask
    sub8 = lax.broadcasted_iota(jnp.int32, (8, cols), 0)
    edge[0, 0] = jnp.where(sub8 < 4, masked_depth[:8], pltpu.roll(mask[:8], 4, 0))
    edge[0, 1] = jnp.where(sub8 >= 4, masked_depth[rows - 8 :], pltpu.roll(mask[rows - 8 :], 4, 0))
    stage_sides(0, (masked_depth, mask))

    pl.semaphore_wait(barrier, peers - 1)
    start_halo(0)

    for get in gets[2:5]:
        get.wait()
    wet = wet_ref[...]

    def add_levels(step, total):
        for j in range(GROUP):
            k = step * GROUP + j
            total = total + jnp.where(k < wet, spacing[k] * heat[k].astype(jnp.float32), 0.0)
        return total

    zero = jnp.zeros((rows, cols), jnp.float32)
    total = lax.fori_loop(0, levels // GROUP, add_levels, zero)
    forcing = mask * total / math.sqrt(levels)
    ext[2, :rows, :cols] = forcing
    edge[1, 0] = forcing[:8]
    edge[1, 1] = forcing[rows - 8 :]
    stage_sides(1, (forcing,))
    start_halo(1)

    wait_halo(0)
    from_n, from_s = land_edge[0, 0], land_edge[0, 1]
    ext[0, rows:, :cols] = jnp.where(sub8 < 4, from_s, from_n)
    ext[1, rows:, :cols] = pltpu.roll(jnp.where(sub8 >= 4, from_s, from_n), 4, 0)
    widen_sides(0, 0, 0)
    widen_sides(0, 1, 1)
    e, m = ext[0], ext[1]
    half_e, half_m = 0.5 * e, 0.5 * m
    centre = SURFACE + (half_e * spread(m) + half_m * spread(e))
    ext[3] = centre
    bound = jnp.max(2.0 * centre[:rows, :cols] - SURFACE, axis=0, keepdims=True)
    local = bound[:, :128]
    for start in range(128, cols, 128):
        local = jnp.maximum(local, bound[:, start : start + 128])
    maxima[0] = local

    def tell(i):
        pltpu.make_async_remote_copy(
            src_ref=maxima.at[0],
            dst_ref=maxima.at[i],
            send_sem=max_send,
            recv_sem=max_recv,
            device_id=peer(i),
            device_id_type=MESH,
        ).start()

    for_peers(tell)
    others = maxima.at[pl.ds(1, peers - 1)]

    gets[5].wait()

    def eliminate(k, carry, coupling):
        ratio, value, above = carry
        inverse = 1.0 / (spacing[k] + coupling + above * (1.0 - ratio))
        source = spacing[k] * heat[k].astype(jnp.float32)
        ratio = coupling * inverse
        value = (source + above * value) * inverse
        ratios[k] = ratio
        values[k] = value
        return ratio, value, coupling

    def forward(step, carry):
        for j in range(GROUP):
            k = step * GROUP + j
            coupling = jnp.where(k + 1 < wet_ref[...], cond[k].astype(jnp.float32), 0.0)
            carry = eliminate(k, carry, coupling)
        return carry

    steps = (levels - 1) // GROUP
    carry = lax.fori_loop(0, steps, forward, (zero, zero, zero))
    for k in range(steps * GROUP, levels):
        coupling = zero
        if k < levels - 1:
            coupling = jnp.where(k + 1 < wet_ref[...], cond[k].astype(jnp.float32), 0.0)
        carry = eliminate(k, carry, coupling)

    wait_halo(1)
    ext[2, rows:, :cols] = jnp.where(sub8 < 4, land_edge[1, 1], land_edge[1, 0])
    widen_sides(1, 0, 2)

    pltpu.make_async_copy(others, others, max_recv).wait()
    top = jnp.max(jnp.max(maxima[...], axis=0), axis=1, keepdims=True)

    theta = 0.5 * (top + SURFACE)
    delta = 0.5 * (top - SURFACE)
    sigma = theta / delta
    e, m, residual, centre = ext[0], ext[1], ext[2], ext[3]
    half_e, half_m = 0.5 * e, 0.5 * m
    direction = residual * (1.0 / theta)
    recur = 1.0 / sigma
    result = jnp.zeros_like(residual)
    for _ in range(ITERS):
        result = result + direction
        image = centre * direction - (
            half_e * spread(m * direction) + half_m * spread(e * direction)
        )
        residual = residual - image
        recur_next = 1.0 / (2.0 * sigma - recur)
        direction = (recur_next * recur) * direction + (2.0 * recur_next / delta) * residual
        recur = recur_next
    height_ref[...] = (result + direction)[:rows, :cols]

    end_halo(0)
    end_halo(1)
    pltpu.make_async_copy(others, others, max_send).wait()


def finish(ratios, values, height, heat_out, height_out, heat, sem):
    levels, rows, cols = values.shape
    parts = sem.shape[0] - 1
    per = levels // parts
    puts = [pltpu.make_async_copy(height, height_out, sem.at[parts])]
    puts[0].start()
    carry = jnp.zeros((rows, cols), jnp.float32)
    for part in reversed(range(parts)):
        for k in reversed(range(part * per, (part + 1) * per)):
            carry = values[k] + ratios[k] * carry
            heat[k] = carry
        span = pl.ds(part * per, per)
        puts.append(pltpu.make_async_copy(heat.at[span], heat_out.at[span], sem.at[part]))
        puts[-1].start()
    for put in puts:
        put.wait()


def local(n_row, n_col, heat, cond, spacing, wet, water, depth):
    levels, rows, cols = heat.shape
    f32 = jnp.float32
    parts = 6
    vmem = pl.BlockSpec(memory_space=pltpu.VMEM)
    hbm = pl.BlockSpec(memory_space=pltpu.HBM)
    dma = pltpu.SemaphoreType.DMA
    column = jax.ShapeDtypeStruct((levels, rows, cols), f32)
    surface = jax.ShapeDtypeStruct((rows, cols), f32)
    held = [
        pltpu.with_memory_space_constraint(x, pltpu.HBM)
        for x in (heat, cond, spacing, wet, water, depth)
    ]
    ratios, values, height = pl.pallas_call(
        functools.partial(kernel, n_row, n_col),
        out_shape=(column, column, surface),
        in_specs=[hbm] * 6,
        out_specs=(vmem, vmem, vmem),
        scratch_shapes=[
            pltpu.VMEM((levels, rows, cols), heat.dtype),
            pltpu.VMEM((levels - 1, rows, cols), cond.dtype),
            pltpu.SMEM((levels,), f32),
            pltpu.VMEM((rows, cols), wet.dtype),
            pltpu.VMEM((rows, cols), water.dtype),
            pltpu.VMEM((rows, cols), f32),
            pltpu.VMEM((4, rows + 8, cols + 128), f32),
            pltpu.VMEM((2, 2, 8, cols), f32),
            pltpu.VMEM((2, 2, 8, 128), f32),
            pltpu.VMEM((2, 2, 8, cols), f32),
            pltpu.VMEM((2, 6, 8, 128), f32),
            pltpu.VMEM((n_row * n_col, 1, 128), f32),
            dma((6,)),
            dma((2, 8)),
            dma((2, 8)),
            dma(()),
            dma(()),
        ],
        compiler_params=pltpu.CompilerParams(
            collective_id=0, has_side_effects=True, vmem_limit_bytes=GRANT
        ),
    )(*held)
    return pl.pallas_call(
        finish,
        out_shape=(column, surface),
        in_specs=[vmem, vmem, vmem],
        out_specs=(hbm, hbm),
        scratch_shapes=[pltpu.VMEM((levels, rows, cols), f32), dma((parts + 1,))],
        compiler_params=pltpu.CompilerParams(has_side_effects=True, vmem_limit_bytes=GRANT),
    )(ratios, values, height)


def solution(mesh):
    placed = (
        P(None, "row", "col"),
        P(None, "row", "col"),
        P(),
        P("row", "col"),
        P("row", "col"),
        P("row", "col"),
    )
    return jax.shard_map(
        functools.partial(local, mesh.shape["row"], mesh.shape["col"]),
        mesh=mesh,
        in_specs=placed,
        out_specs=(P(None, "row", "col"), P("row", "col")),
        check_vma=False,
    )
```

```python
import functools
import math

import jax
import jax.numpy as jnp
from jax import lax
from jax.experimental import pallas as pl
from jax.experimental.pallas import tpu as pltpu
from jax.sharding import PartitionSpec as P

ITERS = 4
SURFACE = 0.5
MESH = pl.DeviceIdType.MESH
GROUP = 4
GRANT = 32 * 1024 * 1024
SLOT = 8


def spread(field):
    rows, lanes = field.shape
    t = pltpu.roll(field, 1, 0) + pltpu.roll(field, rows - 1, 0)
    h = field + 0.5 * t
    return t + (pltpu.roll(h, 1, 1) + pltpu.roll(h, lanes - 1, 1))


def shift(block, by):
    lanes = block.shape[1]
    by = by % lanes
    return block if by == 0 else pltpu.roll(block, by, 1)


def pack_west(blocks):
    lane = lax.broadcasted_iota(jnp.int32, blocks[0].shape, 1)
    out = blocks[0]
    for slot in range(1, len(blocks)):
        out = jnp.where(lane >= SLOT * slot, shift(blocks[slot], SLOT * slot), out)
    return out


def pack_east(blocks):
    lane = lax.broadcasted_iota(jnp.int32, blocks[0].shape, 1)
    out = blocks[0]
    for slot in range(1, len(blocks)):
        out = jnp.where(lane < 128 - SLOT * slot, shift(blocks[slot], -SLOT * slot), out)
    return out


def kernel(
    n_row,
    n_col,
    heat_hbm,
    cond_hbm,
    spacing_hbm,
    wet_hbm,
    water_hbm,
    depth_hbm,
    ratios,
    values,
    height_ref,
    heat,
    cond,
    spacing,
    wet_ref,
    water_ref,
    depth_ref,
    ext,
    edge,
    side,
    land_edge,
    land_side,
    maxima,
    in_sem,
    send_sem,
    recv_sem,
    max_send,
    max_recv,
):
    levels, rows, cols = heat.shape
    half = cols - 128
    tiles = rows // 8
    row, col = lax.axis_index("row"), lax.axis_index("col")
    north, south = row > 0, row < n_row - 1
    up, down = lax.rem(row + n_row - 1, n_row), lax.rem(row + 1, n_row)
    west, east = lax.rem(col + n_col - 1, n_col), lax.rem(col + 1, n_col)

    pairs = (
        (water_hbm, water_ref),
        (depth_hbm, depth_ref),
        (wet_hbm, wet_ref),
        (spacing_hbm, spacing),
        (heat_hbm, heat),
        (cond_hbm, cond),
    )
    gets = [pltpu.make_async_copy(a, b, in_sem.at[i]) for i, (a, b) in enumerate(pairs)]
    for get in gets:
        get.start()

    barrier = pltpu.get_barrier_semaphore()

    def greet(r, c):
        pl.semaphore_signal(barrier, inc=1, device_id=(r, c), device_id_type=MESH)

    def peer(i):
        return lax.rem(row + i // n_col, n_row), lax.rem(col + lax.rem(i, n_col), n_col)

    peers = n_row * n_col

    def for_peers(act):
        if peers <= 64:
            for i in range(1, peers):
                act(jnp.int32(i))
        else:
            lax.fori_loop(1, peers, lambda i, none: (act(i), none)[1], None)

    for_peers(lambda i: greet(*peer(i)))

    @pl.when(jnp.logical_not(north))
    def _():
        for kind in range(1):
            for place in (2, 3):
                land_side[kind, place] = jnp.zeros((8, 128), jnp.float32)
            land_edge[kind, 0] = jnp.zeros((16, cols), jnp.float32)

    @pl.when(jnp.logical_not(south))
    def _():
        for kind in range(1):
            for place in (4, 5):
                land_side[kind, place] = jnp.zeros((8, 128), jnp.float32)
            land_edge[kind, 1] = jnp.zeros((16, cols), jnp.float32)

    def halo_copies(kind):
        def remote(src, dst, slot, target):
            return pltpu.make_async_remote_copy(
                src_ref=src,
                dst_ref=dst,
                send_sem=send_sem.at[kind, slot],
                recv_sem=recv_sem.at[kind, slot],
                device_id=target,
                device_id_type=MESH,
            )

        from_west, from_east = side.at[kind, 0], side.at[kind, 1]
        northward = (
            remote(edge.at[kind, 0], land_edge.at[kind, 1], 0, (up, col)),
            remote(from_west, land_side.at[kind, 5], 1, (up, west)),
            remote(from_east, land_side.at[kind, 4], 2, (up, east)),
        )
        southward = (
            remote(edge.at[kind, 1], land_edge.at[kind, 0], 3, (down, col)),
            remote(from_west, land_side.at[kind, 3], 4, (down, west)),
            remote(from_east, land_side.at[kind, 2], 5, (down, east)),
        )
        sideways = (
            remote(from_west, land_side.at[kind, 1], 6, (row, west)),
            remote(from_east, land_side.at[kind, 0], 7, (row, east)),
        )
        return northward, southward, sideways

    def start_halo(kind):
        northward, southward, sideways = halo_copies(kind)

        @pl.when(north)
        def _():
            for copy in northward:
                copy.start()

        @pl.when(south)
        def _():
            for copy in southward:
                copy.start()

        for copy in sideways:
            copy.start()

    def wait_halo(kind):
        northward, southward, sideways = halo_copies(kind)

        @pl.when(south)
        def _():
            for copy in northward:
                copy.wait_recv()

        @pl.when(north)
        def _():
            for copy in southward:
                copy.wait_recv()

        for copy in sideways:
            copy.wait_recv()

    def end_halo(kind):
        northward, southward, sideways = halo_copies(kind)

        @pl.when(north)
        def _():
            for copy in northward:
                copy.wait_send()

        @pl.when(south)
        def _():
            for copy in southward:
                copy.wait_send()

        for copy in sideways:
            copy.wait_send()

    def stage_sides(kind, fields):
        blocks = [f[8 * t : 8 * t + 8, :128] for f in fields for t in range(tiles)]
        side[kind, 0] = pack_west(blocks)
        blocks = [f[8 * t : 8 * t + 8, half:] for f in fields for t in range(tiles)]
        side[kind, 1] = pack_east(blocks)

    sub_c = lax.broadcasted_iota(jnp.int32, (8, 128), 0)
    lane_c = lax.broadcasted_iota(jnp.int32, (8, 128), 1)

    def widen_sides(kind, slot, target):
        w, e, nw, ne, sw, se = (land_side[kind, place] for place in range(6))
        for t in range(tiles):
            by = SLOT * (slot * tiles + t)
            ext[target, pl.ds(8 * t, 8), cols:] = jnp.where(lane_c < 64, shift(e, -by), shift(w, by))
        first, last = SLOT * slot * tiles, SLOT * (slot * tiles + tiles - 1)
        above = jnp.where(lane_c < 64, shift(ne, -last), shift(nw, last))
        below = jnp.where(lane_c < 64, shift(se, -first), shift(sw, first))
        ext[target, rows:, cols:] = jnp.where(sub_c < 4, below, above)

    gets[0].wait()
    gets[1].wait()
    mask = water_ref[...].astype(jnp.float32)
    masked_depth = mask * depth_ref[...]
    ext[0, :rows, :cols] = masked_depth
    ext[1, :rows, :cols] = mask
    sub8 = lax.broadcasted_iota(jnp.int32, (8, cols), 0)
    for get in gets[2:5]:
        get.wait()
    wet = wet_ref[...]

    def add_levels(step, total):
        for j in range(GROUP):
            k = step * GROUP + j
            total = total + jnp.where(k < wet, spacing[k] * heat[k].astype(jnp.float32), 0.0)
        return total

    zero = jnp.zeros((rows, cols), jnp.float32)
    total = lax.fori_loop(0, levels // GROUP, add_levels, zero)
    forcing = mask * total / math.sqrt(levels)
    ext[2, :rows, :cols] = forcing
    edge[0, 0, :8] = jnp.where(sub8 < 4, masked_depth[:8], pltpu.roll(mask[:8], 4, 0))
    edge[0, 0, 8:] = forcing[:8]
    edge[0, 1, :8] = jnp.where(
        sub8 >= 4, masked_depth[rows - 8 :], pltpu.roll(mask[rows - 8 :], 4, 0)
    )
    edge[0, 1, 8:] = forcing[rows - 8 :]
    stage_sides(0, (masked_depth, mask, forcing))
    pl.semaphore_wait(barrier, peers - 1)
    start_halo(0)

    gets[5].wait()

    def eliminate(k, carry, coupling):
        ratio, value, above = carry
        inverse = 1.0 / (spacing[k] + coupling + above * (1.0 - ratio))
        source = spacing[k] * heat[k].astype(jnp.float32)
        ratio = coupling * inverse
        value = (source + above * value) * inverse
        ratios[k] = ratio
        values[k] = value
        return ratio, value, coupling

    def forward(step, carry):
        for j in range(GROUP):
            k = step * GROUP + j
            coupling = jnp.where(k + 1 < wet_ref[...], cond[k].astype(jnp.float32), 0.0)
            carry = eliminate(k, carry, coupling)
        return carry

    steps = (levels - 1) // GROUP
    carry = lax.fori_loop(0, steps // 2, forward, (zero, zero, zero))

    wait_halo(0)
    from_n, from_s = land_edge[0, 0, :8], land_edge[0, 1, :8]
    ext[0, rows:, :cols] = jnp.where(sub8 < 4, from_s, from_n)
    ext[1, rows:, :cols] = pltpu.roll(jnp.where(sub8 >= 4, from_s, from_n), 4, 0)
    widen_sides(0, 0, 0)
    widen_sides(0, 1, 1)
    e, m = ext[0], ext[1]
    half_e, half_m = 0.5 * e, 0.5 * m
    centre = SURFACE + (half_e * spread(m) + half_m * spread(e))
    ext[3] = centre
    bound = jnp.max(2.0 * centre[:rows, :cols] - SURFACE, axis=0, keepdims=True)
    local = bound[:, :128]
    for start in range(128, cols, 128):
        local = jnp.maximum(local, bound[:, start : start + 128])
    maxima[0] = local

    def tell(i):
        pltpu.make_async_remote_copy(
            src_ref=maxima.at[0],
            dst_ref=maxima.at[i],
            send_sem=max_send,
            recv_sem=max_recv,
            device_id=peer(i),
            device_id_type=MESH,
        ).start()

    for_peers(tell)
    others = maxima.at[pl.ds(1, peers - 1)]

    carry = lax.fori_loop(steps // 2, steps, forward, carry)
    for k in range(steps * GROUP, levels):
        coupling = zero
        if k < levels - 1:
            coupling = jnp.where(k + 1 < wet_ref[...], cond[k].astype(jnp.float32), 0.0)
        carry = eliminate(k, carry, coupling)

    ext[2, rows:, :cols] = jnp.where(sub8 < 4, land_edge[0, 1, 8:], land_edge[0, 0, 8:])
    widen_sides(0, 2, 2)

    pltpu.make_async_copy(others, others, max_recv).wait()
    top = jnp.max(jnp.max(maxima[...], axis=0), axis=1, keepdims=True)

    theta = 0.5 * (top + SURFACE)
    delta = 0.5 * (top - SURFACE)
    sigma = theta / delta
    e, m, residual, centre = ext[0], ext[1], ext[2], ext[3]
    half_e, half_m = 0.5 * e, 0.5 * m
    direction = residual * (1.0 / theta)
    recur = 1.0 / sigma
    result = jnp.zeros_like(residual)
    for _ in range(ITERS):
        result = result + direction
        image = centre * direction - (
            half_e * spread(m * direction) + half_m * spread(e * direction)
        )
        residual = residual - image
        recur_next = 1.0 / (2.0 * sigma - recur)
        direction = (recur_next * recur) * direction + (2.0 * recur_next / delta) * residual
        recur = recur_next
    height_ref[...] = (result + direction)[:rows, :cols]

    end_halo(0)
    pltpu.make_async_copy(others, others, max_send).wait()


def finish(ratios, values, height, heat_out, height_out, heat, sem):
    levels, rows, cols = values.shape
    parts = sem.shape[0] - 1
    per = levels // parts
    puts = [pltpu.make_async_copy(height, height_out, sem.at[parts])]
    puts[0].start()
    carry = jnp.zeros((rows, cols), jnp.float32)
    for part in reversed(range(parts)):
        for k in reversed(range(part * per, (part + 1) * per)):
            carry = values[k] + ratios[k] * carry
            heat[k] = carry
        span = pl.ds(part * per, per)
        puts.append(pltpu.make_async_copy(heat.at[span], heat_out.at[span], sem.at[part]))
        puts[-1].start()
    for put in puts:
        put.wait()


def local(n_row, n_col, heat, cond, spacing, wet, water, depth):
    levels, rows, cols = heat.shape
    f32 = jnp.float32
    parts = 6
    vmem = pl.BlockSpec(memory_space=pltpu.VMEM)
    hbm = pl.BlockSpec(memory_space=pltpu.HBM)
    dma = pltpu.SemaphoreType.DMA
    column = jax.ShapeDtypeStruct((levels, rows, cols), f32)
    surface = jax.ShapeDtypeStruct((rows, cols), f32)
    held = [
        pltpu.with_memory_space_constraint(x, pltpu.HBM)
        for x in (heat, cond, spacing, wet, water, depth)
    ]
    ratios, values, height = pl.pallas_call(
        functools.partial(kernel, n_row, n_col),
        out_shape=(column, column, surface),
        in_specs=[hbm] * 6,
        out_specs=(vmem, vmem, vmem),
        scratch_shapes=[
            pltpu.VMEM((levels, rows, cols), heat.dtype),
            pltpu.VMEM((levels - 1, rows, cols), cond.dtype),
            pltpu.SMEM((levels,), f32),
            pltpu.VMEM((rows, cols), wet.dtype),
            pltpu.VMEM((rows, cols), water.dtype),
            pltpu.VMEM((rows, cols), f32),
            pltpu.VMEM((4, rows + 8, cols + 128), f32),
            pltpu.VMEM((1, 2, 16, cols), f32),
            pltpu.VMEM((1, 2, 8, 128), f32),
            pltpu.VMEM((1, 2, 16, cols), f32),
            pltpu.VMEM((1, 6, 8, 128), f32),
            pltpu.VMEM((n_row * n_col, 1, 128), f32),
            dma((6,)),
            dma((1, 8)),
            dma((1, 8)),
            dma(()),
            dma(()),
        ],
        compiler_params=pltpu.CompilerParams(
            collective_id=0, has_side_effects=True, vmem_limit_bytes=GRANT
        ),
    )(*held)
    return pl.pallas_call(
        finish,
        out_shape=(column, surface),
        in_specs=[vmem, vmem, vmem],
        out_specs=(hbm, hbm),
        scratch_shapes=[pltpu.VMEM((levels, rows, cols), f32), dma((parts + 1,))],
        compiler_params=pltpu.CompilerParams(has_side_effects=True, vmem_limit_bytes=GRANT),
    )(ratios, values, height)


def solution(mesh):
    placed = (
        P(None, "row", "col"),
        P(None, "row", "col"),
        P(),
        P("row", "col"),
        P("row", "col"),
        P("row", "col"),
    )
    return jax.shard_map(
        functools.partial(local, mesh.shape["row"], mesh.shape["col"]),
        mesh=mesh,
        in_specs=placed,
        out_specs=(P(None, "row", "col"), P("row", "col")),
        check_vma=False,
    )
```

```python
import functools
import math

import jax
import jax.numpy as jnp
from jax import lax
from jax.experimental import pallas as pl
from jax.experimental.pallas import tpu as pltpu
from jax.sharding import PartitionSpec as P

ITERS = 4
SURFACE = 0.5
MESH = pl.DeviceIdType.MESH
GROUP = 4
GRANT = 32 * 1024 * 1024
SLOT = 8


def spread(field):
    rows, lanes = field.shape
    t = pltpu.roll(field, 1, 0) + pltpu.roll(field, rows - 1, 0)
    h = field + 0.5 * t
    return t + (pltpu.roll(h, 1, 1) + pltpu.roll(h, lanes - 1, 1))


def shift(block, by):
    lanes = block.shape[1]
    by = by % lanes
    return block if by == 0 else pltpu.roll(block, by, 1)


def pack_west(blocks):
    lane = lax.broadcasted_iota(jnp.int32, blocks[0].shape, 1)
    out = blocks[0]
    for slot in range(1, len(blocks)):
        out = jnp.where(lane >= SLOT * slot, shift(blocks[slot], SLOT * slot), out)
    return out


def pack_east(blocks):
    lane = lax.broadcasted_iota(jnp.int32, blocks[0].shape, 1)
    out = blocks[0]
    for slot in range(1, len(blocks)):
        out = jnp.where(lane < 128 - SLOT * slot, shift(blocks[slot], -SLOT * slot), out)
    return out


def kernel(
    n_row,
    n_col,
    heat_hbm,
    cond_hbm,
    spacing_hbm,
    wet_hbm,
    water_hbm,
    depth_hbm,
    ratios,
    values,
    height_ref,
    heat,
    cond,
    spacing,
    wet_ref,
    water_ref,
    depth_ref,
    ext,
    edge,
    side,
    land_edge,
    land_side,
    maxima,
    in_sem,
    send_sem,
    recv_sem,
    max_send,
    max_recv,
):
    levels, rows, cols = heat.shape
    half = cols - 128
    tiles = rows // 8
    row, col = lax.axis_index("row"), lax.axis_index("col")
    north, south = row > 0, row < n_row - 1
    up, down = lax.rem(row + n_row - 1, n_row), lax.rem(row + 1, n_row)
    west, east = lax.rem(col + n_col - 1, n_col), lax.rem(col + 1, n_col)

    pairs = (
        (water_hbm, water_ref),
        (depth_hbm, depth_ref),
        (wet_hbm, wet_ref),
        (spacing_hbm, spacing),
        (heat_hbm, heat),
        (cond_hbm, cond),
    )
    gets = [pltpu.make_async_copy(a, b, in_sem.at[i]) for i, (a, b) in enumerate(pairs)]
    for get in gets:
        get.start()

    barrier = pltpu.get_barrier_semaphore()

    def greet(r, c):
        pl.semaphore_signal(barrier, inc=1, device_id=(r, c), device_id_type=MESH)

    def peer(i):
        return lax.rem(row + i // n_col, n_row), lax.rem(col + lax.rem(i, n_col), n_col)

    peers = n_row * n_col

    def for_peers(act):
        if peers <= 64:
            for i in range(1, peers):
                act(jnp.int32(i))
        else:
            lax.fori_loop(1, peers, lambda i, none: (act(i), none)[1], None)

    for_peers(lambda i: greet(*peer(i)))

    @pl.when(jnp.logical_not(north))
    def _():
        for kind in range(1):
            for place in (2, 3):
                land_side[kind, place] = jnp.zeros((8, 128), jnp.float32)
            land_edge[kind, 0] = jnp.zeros((12, cols), jnp.float32)

    @pl.when(jnp.logical_not(south))
    def _():
        for kind in range(1):
            for place in (4, 5):
                land_side[kind, place] = jnp.zeros((8, 128), jnp.float32)
            land_edge[kind, 1] = jnp.zeros((12, cols), jnp.float32)

    def halo_copies(kind):
        def remote(src, dst, slot, target):
            return pltpu.make_async_remote_copy(
                src_ref=src,
                dst_ref=dst,
                send_sem=send_sem.at[kind, slot],
                recv_sem=recv_sem.at[kind, slot],
                device_id=target,
                device_id_type=MESH,
            )

        from_west, from_east = side.at[kind, 0], side.at[kind, 1]
        upper, lower = pl.ds(0, 4), pl.ds(4, 4)

        def corner(src, place, rows_sent, slot, target):
            return remote(
                src.at[rows_sent], land_side.at[kind, place, rows_sent], slot, target
            )

        northward = (
            remote(edge.at[kind, 0], land_edge.at[kind, 1], 0, (up, col)),
            corner(from_west, 5, upper, 1, (up, west)),
            corner(from_east, 4, upper, 2, (up, east)),
        )
        southward = (
            remote(edge.at[kind, 1], land_edge.at[kind, 0], 3, (down, col)),
            corner(from_west, 3, lower, 4, (down, west)),
            corner(from_east, 2, lower, 5, (down, east)),
        )
        sideways = (
            remote(from_west, land_side.at[kind, 1], 6, (row, west)),
            remote(from_east, land_side.at[kind, 0], 7, (row, east)),
        )
        return northward, southward, sideways

    def start_halo(kind):
        northward, southward, sideways = halo_copies(kind)

        @pl.when(north)
        def _():
            for copy in northward:
                copy.start()

        @pl.when(south)
        def _():
            for copy in southward:
                copy.start()

        for copy in sideways:
            copy.start()

    def wait_halo(kind):
        northward, southward, sideways = halo_copies(kind)

        @pl.when(south)
        def _():
            for copy in northward:
                copy.wait_recv()

        @pl.when(north)
        def _():
            for copy in southward:
                copy.wait_recv()

        for copy in sideways:
            copy.wait_recv()

    def end_halo(kind):
        northward, southward, sideways = halo_copies(kind)

        @pl.when(north)
        def _():
            for copy in northward:
                copy.wait_send()

        @pl.when(south)
        def _():
            for copy in southward:
                copy.wait_send()

        for copy in sideways:
            copy.wait_send()

    def stage_sides(kind, fields):
        blocks = [f[8 * t : 8 * t + 8, :128] for f in fields for t in range(tiles)]
        side[kind, 0] = pack_west(blocks)
        blocks = [f[8 * t : 8 * t + 8, half:] for f in fields for t in range(tiles)]
        side[kind, 1] = pack_east(blocks)

    sub_c = lax.broadcasted_iota(jnp.int32, (8, 128), 0)
    lane_c = lax.broadcasted_iota(jnp.int32, (8, 128), 1)

    def widen_sides(kind, slot, target):
        w, e = land_side[kind, 0], land_side[kind, 1]
        a_w = jnp.concatenate([land_side[kind, 4, :4], land_side[kind, 2, 4:]], axis=0)
        a_e = jnp.concatenate([land_side[kind, 5, :4], land_side[kind, 3, 4:]], axis=0)
        for t in range(tiles):
            by = SLOT * (slot * tiles + t)
            ext[target, pl.ds(8 * t, 8), cols:] = jnp.where(lane_c < 64, shift(e, -by), shift(w, by))
        first, last = SLOT * slot * tiles, SLOT * (slot * tiles + tiles - 1)
        above = jnp.where(lane_c < 64, shift(a_e, -last), shift(a_w, last))
        below = jnp.where(lane_c < 64, shift(a_e, -first), shift(a_w, first))
        ext[target, rows:, cols:] = jnp.where(sub_c < 4, below, above)

    gets[0].wait()
    gets[1].wait()
    mask = water_ref[...].astype(jnp.float32)
    masked_depth = mask * depth_ref[...]
    ext[0, :rows, :cols] = masked_depth
    ext[1, :rows, :cols] = mask
    sub8 = lax.broadcasted_iota(jnp.int32, (8, cols), 0)
    for get in gets[2:5]:
        get.wait()
    wet = wet_ref[...]

    def add_levels(step, total):
        for j in range(GROUP):
            k = step * GROUP + j
            total = total + jnp.where(k < wet, spacing[k] * heat[k].astype(jnp.float32), 0.0)
        return total

    zero = jnp.zeros((rows, cols), jnp.float32)
    total = lax.fori_loop(0, levels // GROUP, add_levels, zero)
    forcing = mask * total / math.sqrt(levels)
    ext[2, :rows, :cols] = forcing
    edge[0, 0, :8] = jnp.where(sub8 < 4, masked_depth[:8], pltpu.roll(mask[:8], 4, 0))
    edge[0, 0, 8:] = forcing[:4]
    edge[0, 1, :8] = jnp.where(
        sub8 >= 4, masked_depth[rows - 8 :], pltpu.roll(mask[rows - 8 :], 4, 0)
    )
    edge[0, 1, 8:] = forcing[rows - 4 :]
    stage_sides(0, (masked_depth, mask, forcing))
    pl.semaphore_wait(barrier, peers - 1)
    start_halo(0)

    gets[5].wait()

    def eliminate(k, carry, coupling):
        ratio, value, above = carry
        inverse = 1.0 / (spacing[k] + coupling + above * (1.0 - ratio))
        source = spacing[k] * heat[k].astype(jnp.float32)
        ratio = coupling * inverse
        value = (source + above * value) * inverse
        ratios[k] = ratio
        values[k] = value
        return ratio, value, coupling

    def forward(step, carry):
        for j in range(GROUP):
            k = step * GROUP + j
            coupling = jnp.where(k + 1 < wet_ref[...], cond[k].astype(jnp.float32), 0.0)
            carry = eliminate(k, carry, coupling)
        return carry

    steps = (levels - 1) // GROUP
    carry = lax.fori_loop(0, steps // 2, forward, (zero, zero, zero))

    wait_halo(0)
    from_n, from_s = land_edge[0, 0, :8], land_edge[0, 1, :8]
    ext[0, rows:, :cols] = jnp.where(sub8 < 4, from_s, from_n)
    ext[1, rows:, :cols] = pltpu.roll(jnp.where(sub8 >= 4, from_s, from_n), 4, 0)
    widen_sides(0, 0, 0)
    widen_sides(0, 1, 1)
    e, m = ext[0], ext[1]
    half_e, half_m = 0.5 * e, 0.5 * m
    centre = SURFACE + (half_e * spread(m) + half_m * spread(e))
    ext[3] = centre
    bound = jnp.max(2.0 * centre[:rows, :cols] - SURFACE, axis=0, keepdims=True)
    local = bound[:, :128]
    for start in range(128, cols, 128):
        local = jnp.maximum(local, bound[:, start : start + 128])
    maxima[0] = local

    def tell(i):
        pltpu.make_async_remote_copy(
            src_ref=maxima.at[0],
            dst_ref=maxima.at[i],
            send_sem=max_send,
            recv_sem=max_recv,
            device_id=peer(i),
            device_id_type=MESH,
        ).start()

    for_peers(tell)
    others = maxima.at[pl.ds(1, peers - 1)]

    carry = lax.fori_loop(steps // 2, steps, forward, carry)
    for k in range(steps * GROUP, levels):
        coupling = zero
        if k < levels - 1:
            coupling = jnp.where(k + 1 < wet_ref[...], cond[k].astype(jnp.float32), 0.0)
        carry = eliminate(k, carry, coupling)

    ext[2, rows : rows + 4, :cols] = land_edge[0, 1, 8:]
    ext[2, rows + 4 :, :cols] = land_edge[0, 0, 8:]
    widen_sides(0, 2, 2)

    e, m, residual, centre = ext[0], ext[1], ext[2], ext[3]
    half_e, half_m = 0.5 * e, 0.5 * m

    def operate(v):
        return centre * v - (half_e * spread(m * v) + half_m * spread(e * v))

    once = operate(residual)
    twice = operate(once)

    pltpu.make_async_copy(others, others, max_recv).wait()
    top = jnp.max(jnp.max(maxima[...], axis=0), axis=1, keepdims=True)

    theta = 0.5 * (top + SURFACE)
    delta = 0.5 * (top - SURFACE)
    sigma = theta / delta
    by_theta = 1.0 / theta
    direction = residual * by_theta
    recur = 1.0 / sigma
    result = jnp.zeros_like(residual)
    for step in range(ITERS):
        result = result + direction
        if step == 0:
            image = once * by_theta
        elif step == 1:
            image = keep * (once * by_theta) + gain * (once - twice * by_theta)
        else:
            image = operate(direction)
        residual = residual - image
        recur_next = 1.0 / (2.0 * sigma - recur)
        keep, gain = recur_next * recur, 2.0 * recur_next / delta
        direction = keep * direction + gain * residual
        recur = recur_next
    height_ref[...] = (result + direction)[:rows, :cols]

    end_halo(0)
    pltpu.make_async_copy(others, others, max_send).wait()


def finish(ratios, values, height, heat_out, height_out, heat, sem):
    levels, rows, cols = values.shape
    parts = sem.shape[0] - 1
    per = levels // parts
    puts = [pltpu.make_async_copy(height, height_out, sem.at[parts])]
    puts[0].start()
    carry = jnp.zeros((rows, cols), jnp.float32)
    for part in reversed(range(parts)):
        for k in reversed(range(part * per, (part + 1) * per)):
            carry = values[k] + ratios[k] * carry
            heat[k] = carry
        span = pl.ds(part * per, per)
        puts.append(pltpu.make_async_copy(heat.at[span], heat_out.at[span], sem.at[part]))
        puts[-1].start()
    for put in puts:
        put.wait()


def local(n_row, n_col, heat, cond, spacing, wet, water, depth):
    levels, rows, cols = heat.shape
    f32 = jnp.float32
    parts = 6
    vmem = pl.BlockSpec(memory_space=pltpu.VMEM)
    hbm = pl.BlockSpec(memory_space=pltpu.HBM)
    dma = pltpu.SemaphoreType.DMA
    column = jax.ShapeDtypeStruct((levels, rows, cols), f32)
    surface = jax.ShapeDtypeStruct((rows, cols), f32)
    held = [
        pltpu.with_memory_space_constraint(x, pltpu.HBM)
        for x in (heat, cond, spacing, wet, water, depth)
    ]
    ratios, values, height = pl.pallas_call(
        functools.partial(kernel, n_row, n_col),
        out_shape=(column, column, surface),
        in_specs=[hbm] * 6,
        out_specs=(vmem, vmem, vmem),
        scratch_shapes=[
            pltpu.VMEM((levels, rows, cols), heat.dtype),
            pltpu.VMEM((levels - 1, rows, cols), cond.dtype),
            pltpu.SMEM((levels,), f32),
            pltpu.VMEM((rows, cols), wet.dtype),
            pltpu.VMEM((rows, cols), water.dtype),
            pltpu.VMEM((rows, cols), f32),
            pltpu.VMEM((4, rows + 8, cols + 128), f32),
            pltpu.VMEM((1, 2, 12, cols), f32),
            pltpu.VMEM((1, 2, 8, 128), f32),
            pltpu.VMEM((1, 2, 12, cols), f32),
            pltpu.VMEM((1, 6, 8, 128), f32),
            pltpu.VMEM((n_row * n_col, 1, 128), f32),
            dma((6,)),
            dma((1, 8)),
            dma((1, 8)),
            dma(()),
            dma(()),
        ],
        compiler_params=pltpu.CompilerParams(
            collective_id=0, has_side_effects=True, vmem_limit_bytes=GRANT
        ),
    )(*held)
    return pl.pallas_call(
        finish,
        out_shape=(column, surface),
        in_specs=[vmem, vmem, vmem],
        out_specs=(hbm, hbm),
        scratch_shapes=[pltpu.VMEM((levels, rows, cols), f32), dma((parts + 1,))],
        compiler_params=pltpu.CompilerParams(has_side_effects=True, vmem_limit_bytes=GRANT),
    )(ratios, values, height)


def solution(mesh):
    placed = (
        P(None, "row", "col"),
        P(None, "row", "col"),
        P(),
        P("row", "col"),
        P("row", "col"),
        P("row", "col"),
    )
    return jax.shard_map(
        functools.partial(local, mesh.shape["row"], mesh.shape["col"]),
        mesh=mesh,
        in_specs=placed,
        out_specs=(P(None, "row", "col"), P("row", "col")),
        check_vma=False,
    )
```

```python
import functools
import math

import jax
import jax.numpy as jnp
from jax import lax
from jax.experimental import pallas as pl
from jax.experimental.pallas import tpu as pltpu
from jax.sharding import PartitionSpec as P

ITERS = 4
SURFACE = 0.5
MESH = pl.DeviceIdType.MESH
GROUP = 4
GRANT = 32 * 1024 * 1024
SLOT = 8


def spread(field):
    rows, lanes = field.shape
    t = pltpu.roll(field, 1, 0) + pltpu.roll(field, rows - 1, 0)
    h = field + 0.5 * t
    return t + (pltpu.roll(h, 1, 1) + pltpu.roll(h, lanes - 1, 1))


def shift(block, by):
    lanes = block.shape[1]
    by = by % lanes
    return block if by == 0 else pltpu.roll(block, by, 1)


def pack_west(blocks):
    lane = lax.broadcasted_iota(jnp.int32, blocks[0].shape, 1)
    out = blocks[0]
    for slot in range(1, len(blocks)):
        out = jnp.where(lane >= SLOT * slot, shift(blocks[slot], SLOT * slot), out)
    return out


def pack_east(blocks):
    lane = lax.broadcasted_iota(jnp.int32, blocks[0].shape, 1)
    out = blocks[0]
    for slot in range(1, len(blocks)):
        out = jnp.where(lane < 128 - SLOT * slot, shift(blocks[slot], -SLOT * slot), out)
    return out


def kernel(
    n_row,
    n_col,
    heat_hbm,
    cond_hbm,
    spacing_hbm,
    wet_hbm,
    water_hbm,
    depth_hbm,
    ratios,
    values,
    height_ref,
    heat,
    cond,
    spacing,
    wet_ref,
    water_ref,
    depth_ref,
    ext,
    edge,
    side,
    land_edge,
    land_side,
    maxima,
    in_sem,
    send_sem,
    recv_sem,
    max_send,
    max_recv,
):
    levels, rows, cols = heat.shape
    half = cols - 128
    tiles = rows // 8
    row, col = lax.axis_index("row"), lax.axis_index("col")
    north, south = row > 0, row < n_row - 1
    up, down = lax.rem(row + n_row - 1, n_row), lax.rem(row + 1, n_row)
    west, east = lax.rem(col + n_col - 1, n_col), lax.rem(col + 1, n_col)

    pairs = (
        (water_hbm, water_ref),
        (depth_hbm, depth_ref),
        (wet_hbm, wet_ref),
        (spacing_hbm, spacing),
        (heat_hbm, heat),
        (cond_hbm, cond),
    )
    gets = [pltpu.make_async_copy(a, b, in_sem.at[i]) for i, (a, b) in enumerate(pairs)]
    for get in gets:
        get.start()

    barrier = pltpu.get_barrier_semaphore()

    def greet(r, c):
        pl.semaphore_signal(barrier, inc=1, device_id=(r, c), device_id_type=MESH)

    def peer(i):
        return lax.rem(row + i // n_col, n_row), lax.rem(col + lax.rem(i, n_col), n_col)

    peers = n_row * n_col

    def for_peers(act):
        if peers <= 64:
            for i in range(1, peers):
                act(jnp.int32(i))
        else:
            lax.fori_loop(1, peers, lambda i, none: (act(i), none)[1], None)

    for_peers(lambda i: greet(*peer(i)))

    @pl.when(jnp.logical_not(north))
    def _():
        for kind in range(2):
            for place in (2, 3):
                land_side[kind, place] = jnp.zeros((8, 128), jnp.float32)
            land_edge[kind, 0] = jnp.zeros((8, cols), jnp.float32)

    @pl.when(jnp.logical_not(south))
    def _():
        for kind in range(2):
            for place in (4, 5):
                land_side[kind, place] = jnp.zeros((8, 128), jnp.float32)
            land_edge[kind, 1] = jnp.zeros((8, cols), jnp.float32)

    def halo_copies(kind):
        def remote(src, dst, slot, target):
            return pltpu.make_async_remote_copy(
                src_ref=src,
                dst_ref=dst,
                send_sem=send_sem.at[kind, slot],
                recv_sem=recv_sem.at[kind, slot],
                device_id=target,
                device_id_type=MESH,
            )

        from_west, from_east = side.at[kind, 0], side.at[kind, 1]
        upper, lower = pl.ds(0, 4), pl.ds(4, 4)

        def corner(src, place, rows_sent, slot, target):
            return remote(
                src.at[rows_sent], land_side.at[kind, place, rows_sent], slot, target
            )

        def border(own, place, rows_sent, slot, target):
            if kind == 0:
                return remote(edge.at[0, own], land_edge.at[0, place], slot, target)
            src, dst = edge.at[kind, own, rows_sent], land_edge.at[kind, place, rows_sent]
            return remote(src, dst, slot, target)

        northward = (
            border(0, 1, upper, 0, (up, col)),
            corner(from_west, 5, upper, 1, (up, west)),
            corner(from_east, 4, upper, 2, (up, east)),
        )
        southward = (
            border(1, 0, lower, 3, (down, col)),
            corner(from_west, 3, lower, 4, (down, west)),
            corner(from_east, 2, lower, 5, (down, east)),
        )
        sideways = (
            remote(from_west, land_side.at[kind, 1], 6, (row, west)),
            remote(from_east, land_side.at[kind, 0], 7, (row, east)),
        )
        return northward, southward, sideways

    def start_halo(kind):
        northward, southward, sideways = halo_copies(kind)

        @pl.when(north)
        def _():
            for copy in northward:
                copy.start()

        @pl.when(south)
        def _():
            for copy in southward:
                copy.start()

        for copy in sideways:
            copy.start()

    def wait_halo(kind):
        northward, southward, sideways = halo_copies(kind)

        @pl.when(south)
        def _():
            for copy in northward:
                copy.wait_recv()

        @pl.when(north)
        def _():
            for copy in southward:
                copy.wait_recv()

        for copy in sideways:
            copy.wait_recv()

    def end_halo(kind):
        northward, southward, sideways = halo_copies(kind)

        @pl.when(north)
        def _():
            for copy in northward:
                copy.wait_send()

        @pl.when(south)
        def _():
            for copy in southward:
                copy.wait_send()

        for copy in sideways:
            copy.wait_send()

    def stage_sides(kind, fields):
        blocks = [f[8 * t : 8 * t + 8, :128] for f in fields for t in range(tiles)]
        side[kind, 0] = pack_west(blocks)
        blocks = [f[8 * t : 8 * t + 8, half:] for f in fields for t in range(tiles)]
        side[kind, 1] = pack_east(blocks)

    sub_c = lax.broadcasted_iota(jnp.int32, (8, 128), 0)
    lane_c = lax.broadcasted_iota(jnp.int32, (8, 128), 1)

    def widen_sides(kind, slot, target):
        w, e = land_side[kind, 0], land_side[kind, 1]
        a_w = jnp.concatenate([land_side[kind, 4, :4], land_side[kind, 2, 4:]], axis=0)
        a_e = jnp.concatenate([land_side[kind, 5, :4], land_side[kind, 3, 4:]], axis=0)
        for t in range(tiles):
            by = SLOT * (slot * tiles + t)
            ext[target, pl.ds(8 * t, 8), cols:] = jnp.where(lane_c < 64, shift(e, -by), shift(w, by))
        first, last = SLOT * slot * tiles, SLOT * (slot * tiles + tiles - 1)
        above = jnp.where(lane_c < 64, shift(a_e, -last), shift(a_w, last))
        below = jnp.where(lane_c < 64, shift(a_e, -first), shift(a_w, first))
        ext[target, rows:, cols:] = jnp.where(sub_c < 4, below, above)

    gets[0].wait()
    gets[1].wait()
    mask = water_ref[...].astype(jnp.float32)
    masked_depth = mask * depth_ref[...]
    ext[0, :rows, :cols] = masked_depth
    ext[1, :rows, :cols] = mask
    sub8 = lax.broadcasted_iota(jnp.int32, (8, cols), 0)
    edge[0, 0] = jnp.where(sub8 < 4, masked_depth[:8], pltpu.roll(mask[:8], 4, 0))
    edge[0, 1] = jnp.where(sub8 >= 4, masked_depth[rows - 8 :], pltpu.roll(mask[rows - 8 :], 4, 0))
    stage_sides(0, (masked_depth, mask))
    pl.semaphore_wait(barrier, peers - 1)
    start_halo(0)

    for get in gets[2:5]:
        get.wait()
    wet = wet_ref[...]

    def add_levels(step, total):
        for j in range(GROUP):
            k = step * GROUP + j
            total = total + jnp.where(k < wet, spacing[k] * heat[k].astype(jnp.float32), 0.0)
        return total

    zero = jnp.zeros((rows, cols), jnp.float32)
    total = lax.fori_loop(0, levels // GROUP, add_levels, zero)
    forcing = mask * total / math.sqrt(levels)
    ext[2, :rows, :cols] = forcing
    edge[1, 0] = forcing[:8]
    edge[1, 1] = forcing[rows - 8 :]
    stage_sides(1, (forcing,))
    start_halo(1)

    gets[5].wait()

    def eliminate(k, carry, coupling):
        ratio, value, above = carry
        inverse = 1.0 / (spacing[k] + coupling + above * (1.0 - ratio))
        source = spacing[k] * heat[k].astype(jnp.float32)
        ratio = coupling * inverse
        value = (source + above * value) * inverse
        ratios[k] = ratio
        values[k] = value
        return ratio, value, coupling

    def forward(step, carry):
        for j in range(GROUP):
            k = step * GROUP + j
            coupling = jnp.where(k + 1 < wet_ref[...], cond[k].astype(jnp.float32), 0.0)
            carry = eliminate(k, carry, coupling)
        return carry

    steps = (levels - 1) // GROUP
    carry = lax.fori_loop(0, steps // 4, forward, (zero, zero, zero))

    wait_halo(0)
    from_n, from_s = land_edge[0, 0], land_edge[0, 1]
    ext[0, rows:, :cols] = jnp.where(sub8 < 4, from_s, from_n)
    ext[1, rows:, :cols] = pltpu.roll(jnp.where(sub8 >= 4, from_s, from_n), 4, 0)
    widen_sides(0, 0, 0)
    widen_sides(0, 1, 1)
    e, m = ext[0], ext[1]
    half_e, half_m = 0.5 * e, 0.5 * m
    centre = SURFACE + (half_e * spread(m) + half_m * spread(e))
    ext[3] = centre
    bound = jnp.max(2.0 * centre[:rows, :cols] - SURFACE, axis=0, keepdims=True)
    local = bound[:, :128]
    for start in range(128, cols, 128):
        local = jnp.maximum(local, bound[:, start : start + 128])
    maxima[0] = local

    def tell(i):
        pltpu.make_async_remote_copy(
            src_ref=maxima.at[0],
            dst_ref=maxima.at[i],
            send_sem=max_send,
            recv_sem=max_recv,
            device_id=peer(i),
            device_id_type=MESH,
        ).start()

    for_peers(tell)
    others = maxima.at[pl.ds(1, peers - 1)]

    carry = lax.fori_loop(steps // 4, steps, forward, carry)
    for k in range(steps * GROUP, levels):
        coupling = zero
        if k < levels - 1:
            coupling = jnp.where(k + 1 < wet_ref[...], cond[k].astype(jnp.float32), 0.0)
        carry = eliminate(k, carry, coupling)

    wait_halo(1)
    ext[2, rows : rows + 4, :cols] = land_edge[1, 1, :4]
    ext[2, rows + 4 :, :cols] = land_edge[1, 0, 4:]
    widen_sides(1, 0, 2)

    e, m, residual, centre = ext[0], ext[1], ext[2], ext[3]
    half_e, half_m = 0.5 * e, 0.5 * m

    def operate(v):
        return centre * v - (half_e * spread(m * v) + half_m * spread(e * v))

    once = operate(residual)
    twice = operate(once)

    pltpu.make_async_copy(others, others, max_recv).wait()
    top = jnp.max(jnp.max(maxima[...], axis=0), axis=1, keepdims=True)

    theta = 0.5 * (top + SURFACE)
    delta = 0.5 * (top - SURFACE)
    sigma = theta / delta
    by_theta = 1.0 / theta
    direction = residual * by_theta
    recur = 1.0 / sigma
    result = jnp.zeros_like(residual)
    for step in range(ITERS):
        result = result + direction
        if step == 0:
            image = once * by_theta
        elif step == 1:
            image = keep * (once * by_theta) + gain * (once - twice * by_theta)
        else:
            image = operate(direction)
        residual = residual - image
        recur_next = 1.0 / (2.0 * sigma - recur)
        keep, gain = recur_next * recur, 2.0 * recur_next / delta
        direction = keep * direction + gain * residual
        recur = recur_next
    height_ref[...] = (result + direction)[:rows, :cols]

    end_halo(0)
    end_halo(1)
    pltpu.make_async_copy(others, others, max_send).wait()


def finish(ratios, values, height, heat_out, height_out, heat, sem):
    levels, rows, cols = values.shape
    parts = sem.shape[0] - 1
    per = levels // parts
    puts = [pltpu.make_async_copy(height, height_out, sem.at[parts])]
    puts[0].start()
    carry = jnp.zeros((rows, cols), jnp.float32)
    for part in reversed(range(parts)):
        for k in reversed(range(part * per, (part + 1) * per)):
            carry = values[k] + ratios[k] * carry
            heat[k] = carry
        span = pl.ds(part * per, per)
        puts.append(pltpu.make_async_copy(heat.at[span], heat_out.at[span], sem.at[part]))
        puts[-1].start()
    for put in puts:
        put.wait()


def local(n_row, n_col, heat, cond, spacing, wet, water, depth):
    levels, rows, cols = heat.shape
    f32 = jnp.float32
    parts = 6
    vmem = pl.BlockSpec(memory_space=pltpu.VMEM)
    hbm = pl.BlockSpec(memory_space=pltpu.HBM)
    dma = pltpu.SemaphoreType.DMA
    column = jax.ShapeDtypeStruct((levels, rows, cols), f32)
    surface = jax.ShapeDtypeStruct((rows, cols), f32)
    held = [
        pltpu.with_memory_space_constraint(x, pltpu.HBM)
        for x in (heat, cond, spacing, wet, water, depth)
    ]
    ratios, values, height = pl.pallas_call(
        functools.partial(kernel, n_row, n_col),
        out_shape=(column, column, surface),
        in_specs=[hbm] * 6,
        out_specs=(vmem, vmem, vmem),
        scratch_shapes=[
            pltpu.VMEM((levels, rows, cols), heat.dtype),
            pltpu.VMEM((levels - 1, rows, cols), cond.dtype),
            pltpu.SMEM((levels,), f32),
            pltpu.VMEM((rows, cols), wet.dtype),
            pltpu.VMEM((rows, cols), water.dtype),
            pltpu.VMEM((rows, cols), f32),
            pltpu.VMEM((4, rows + 8, cols + 128), f32),
            pltpu.VMEM((2, 2, 8, cols), f32),
            pltpu.VMEM((2, 2, 8, 128), f32),
            pltpu.VMEM((2, 2, 8, cols), f32),
            pltpu.VMEM((2, 6, 8, 128), f32),
            pltpu.VMEM((n_row * n_col, 1, 128), f32),
            dma((6,)),
            dma((2, 8)),
            dma((2, 8)),
            dma(()),
            dma(()),
        ],
        compiler_params=pltpu.CompilerParams(
            collective_id=0, has_side_effects=True, vmem_limit_bytes=GRANT
        ),
    )(*held)
    return pl.pallas_call(
        finish,
        out_shape=(column, surface),
        in_specs=[vmem, vmem, vmem],
        out_specs=(hbm, hbm),
        scratch_shapes=[pltpu.VMEM((levels, rows, cols), f32), dma((parts + 1,))],
        compiler_params=pltpu.CompilerParams(has_side_effects=True, vmem_limit_bytes=GRANT),
    )(ratios, values, height)


def solution(mesh):
    placed = (
        P(None, "row", "col"),
        P(None, "row", "col"),
        P(),
        P("row", "col"),
        P("row", "col"),
        P("row", "col"),
    )
    return jax.shard_map(
        functools.partial(local, mesh.shape["row"], mesh.shape["col"]),
        mesh=mesh,
        in_specs=placed,
        out_specs=(P(None, "row", "col"), P("row", "col")),
        check_vma=False,
    )
```

```python
import functools
import math

import jax
import jax.numpy as jnp
from jax import lax
from jax.experimental import pallas as pl
from jax.experimental.pallas import tpu as pltpu
from jax.sharding import PartitionSpec as P

ITERS = 4
SURFACE = 0.5
MESH = pl.DeviceIdType.MESH
GROUP = 4
GRANT = 32 * 1024 * 1024
SLOT = 8


def spread(field):
    rows, lanes = field.shape
    t = pltpu.roll(field, 1, 0) + pltpu.roll(field, rows - 1, 0)
    h = field + 0.5 * t
    return t + (pltpu.roll(h, 1, 1) + pltpu.roll(h, lanes - 1, 1))


def shift(block, by):
    lanes = block.shape[1]
    by = by % lanes
    return block if by == 0 else pltpu.roll(block, by, 1)


def pack_west(blocks):
    lane = lax.broadcasted_iota(jnp.int32, blocks[0].shape, 1)
    out = blocks[0]
    for slot in range(1, len(blocks)):
        out = jnp.where(lane >= SLOT * slot, shift(blocks[slot], SLOT * slot), out)
    return out


def pack_east(blocks):
    lane = lax.broadcasted_iota(jnp.int32, blocks[0].shape, 1)
    out = blocks[0]
    for slot in range(1, len(blocks)):
        out = jnp.where(lane < 128 - SLOT * slot, shift(blocks[slot], -SLOT * slot), out)
    return out


def kernel(
    n_row,
    n_col,
    heat_hbm,
    cond_hbm,
    spacing_hbm,
    wet_hbm,
    water_hbm,
    depth_hbm,
    ratios,
    values,
    height_ref,
    heat,
    cond,
    spacing,
    wet_ref,
    water_ref,
    depth_ref,
    ext,
    edge,
    side,
    land_edge,
    land_side,
    maxima,
    in_sem,
    send_sem,
    recv_sem,
    max_send,
    max_recv,
):
    levels, rows, cols = heat.shape
    half = cols - 128
    tiles = rows // 8
    row, col = lax.axis_index("row"), lax.axis_index("col")
    north, south = row > 0, row < n_row - 1
    up, down = lax.rem(row + n_row - 1, n_row), lax.rem(row + 1, n_row)
    west, east = lax.rem(col + n_col - 1, n_col), lax.rem(col + 1, n_col)

    pairs = (
        (water_hbm, water_ref),
        (depth_hbm, depth_ref),
        (wet_hbm, wet_ref),
        (spacing_hbm, spacing),
        (heat_hbm, heat),
        (cond_hbm, cond),
    )
    gets = [pltpu.make_async_copy(a, b, in_sem.at[i]) for i, (a, b) in enumerate(pairs)]
    for get in gets:
        get.start()

    barrier = pltpu.get_barrier_semaphore()

    def greet(r, c):
        pl.semaphore_signal(barrier, inc=1, device_id=(r, c), device_id_type=MESH)

    def peer(i):
        return lax.rem(row + i // n_col, n_row), lax.rem(col + lax.rem(i, n_col), n_col)

    peers = n_row * n_col

    def for_peers(act):
        if peers <= 64:
            for i in range(1, peers):
                act(jnp.int32(i))
        else:
            lax.fori_loop(1, peers, lambda i, none: (act(i), none)[1], None)

    for_peers(lambda i: greet(*peer(i)))

    @pl.when(jnp.logical_not(north))
    def _():
        for kind in range(1):
            for place in (2, 3):
                land_side[kind, place] = jnp.zeros((8, 128), jnp.float32)
            land_edge[kind, 0] = jnp.zeros((12, cols), jnp.float32)

    @pl.when(jnp.logical_not(south))
    def _():
        for kind in range(1):
            for place in (4, 5):
                land_side[kind, place] = jnp.zeros((8, 128), jnp.float32)
            land_edge[kind, 1] = jnp.zeros((12, cols), jnp.float32)

    def halo_copies(kind):
        def remote(src, dst, slot, target):
            return pltpu.make_async_remote_copy(
                src_ref=src,
                dst_ref=dst,
                send_sem=send_sem.at[kind, slot],
                recv_sem=recv_sem.at[kind, slot],
                device_id=target,
                device_id_type=MESH,
            )

        from_west, from_east = side.at[kind, 0], side.at[kind, 1]
        upper, lower = pl.ds(0, 4), pl.ds(4, 4)

        def corner(src, place, rows_sent, slot, target):
            return remote(
                src.at[rows_sent], land_side.at[kind, place, rows_sent], slot, target
            )

        northward = (
            remote(edge.at[kind, 0], land_edge.at[kind, 1], 0, (up, col)),
            corner(from_west, 5, upper, 1, (up, west)),
            corner(from_east, 4, upper, 2, (up, east)),
        )
        southward = (
            remote(edge.at[kind, 1], land_edge.at[kind, 0], 3, (down, col)),
            corner(from_west, 3, lower, 4, (down, west)),
            corner(from_east, 2, lower, 5, (down, east)),
        )
        sideways = (
            remote(from_west, land_side.at[kind, 1], 6, (row, west)),
            remote(from_east, land_side.at[kind, 0], 7, (row, east)),
        )
        return northward, southward, sideways

    def start_halo(kind):
        northward, southward, sideways = halo_copies(kind)

        @pl.when(north)
        def _():
            for copy in northward:
                copy.start()

        @pl.when(south)
        def _():
            for copy in southward:
                copy.start()

        for copy in sideways:
            copy.start()

    def wait_halo(kind):
        northward, southward, sideways = halo_copies(kind)

        @pl.when(south)
        def _():
            for copy in northward:
                copy.wait_recv()

        @pl.when(north)
        def _():
            for copy in southward:
                copy.wait_recv()

        for copy in sideways:
            copy.wait_recv()

    def end_halo(kind):
        northward, southward, sideways = halo_copies(kind)

        @pl.when(north)
        def _():
            for copy in northward:
                copy.wait_send()

        @pl.when(south)
        def _():
            for copy in southward:
                copy.wait_send()

        for copy in sideways:
            copy.wait_send()

    def stage_sides(kind, fields):
        blocks = [f[8 * t : 8 * t + 8, :128] for f in fields for t in range(tiles)]
        side[kind, 0] = pack_west(blocks)
        blocks = [f[8 * t : 8 * t + 8, half:] for f in fields for t in range(tiles)]
        side[kind, 1] = pack_east(blocks)

    sub_c = lax.broadcasted_iota(jnp.int32, (8, 128), 0)
    lane_c = lax.broadcasted_iota(jnp.int32, (8, 128), 1)

    def widen_sides(kind, slot, target):
        w, e = land_side[kind, 0], land_side[kind, 1]
        a_w = jnp.concatenate([land_side[kind, 4, :4], land_side[kind, 2, 4:]], axis=0)
        a_e = jnp.concatenate([land_side[kind, 5, :4], land_side[kind, 3, 4:]], axis=0)
        for t in range(tiles):
            by = SLOT * (slot * tiles + t)
            ext[target, pl.ds(8 * t, 8), cols:] = jnp.where(lane_c < 64, shift(e, -by), shift(w, by))
        first, last = SLOT * slot * tiles, SLOT * (slot * tiles + tiles - 1)
        above = jnp.where(lane_c < 64, shift(a_e, -last), shift(a_w, last))
        below = jnp.where(lane_c < 64, shift(a_e, -first), shift(a_w, first))
        ext[target, rows:, cols:] = jnp.where(sub_c < 4, below, above)

    gets[0].wait()
    gets[1].wait()
    mask = water_ref[...].astype(jnp.float32)
    masked_depth = mask * depth_ref[...]
    ext[0, :rows, :cols] = masked_depth
    ext[1, :rows, :cols] = mask
    sub8 = lax.broadcasted_iota(jnp.int32, (8, cols), 0)
    for get in gets[2:5]:
        get.wait()
    wet = wet_ref[...]

    def add_levels(step, total):
        for j in range(GROUP):
            k = step * GROUP + j
            total = total + jnp.where(k < wet, spacing[k] * heat[k].astype(jnp.float32), 0.0)
        return total

    zero = jnp.zeros((rows, cols), jnp.float32)
    total = lax.fori_loop(0, levels // GROUP, add_levels, zero)
    forcing = mask * total / math.sqrt(levels)
    ext[2, :rows, :cols] = forcing
    edge[0, 0, :8] = jnp.where(sub8 < 4, masked_depth[:8], pltpu.roll(mask[:8], 4, 0))
    edge[0, 0, 8:] = forcing[:4]
    edge[0, 1, :8] = jnp.where(
        sub8 >= 4, masked_depth[rows - 8 :], pltpu.roll(mask[rows - 8 :], 4, 0)
    )
    edge[0, 1, 8:] = forcing[rows - 4 :]
    stage_sides(0, (masked_depth, mask, forcing))
    pl.semaphore_wait(barrier, peers - 1)
    start_halo(0)

    gets[5].wait()

    def eliminate(k, carry, coupling):
        ratio, value, above = carry
        inverse = 1.0 / (spacing[k] + coupling + above * (1.0 - ratio))
        source = spacing[k] * heat[k].astype(jnp.float32)
        ratio = coupling * inverse
        value = (source + above * value) * inverse
        ratios[k] = ratio
        values[k] = value
        return ratio, value, coupling

    def forward(step, carry):
        for j in range(GROUP):
            k = step * GROUP + j
            coupling = jnp.where(k + 1 < wet_ref[...], cond[k].astype(jnp.float32), 0.0)
            carry = eliminate(k, carry, coupling)
        return carry

    steps = (levels - 1) // GROUP
    carry = lax.fori_loop(0, steps // 2, forward, (zero, zero, zero))

    wait_halo(0)
    from_n, from_s = land_edge[0, 0, :8], land_edge[0, 1, :8]
    ext[0, rows:, :cols] = jnp.where(sub8 < 4, from_s, from_n)
    ext[1, rows:, :cols] = pltpu.roll(jnp.where(sub8 >= 4, from_s, from_n), 4, 0)
    widen_sides(0, 0, 0)
    widen_sides(0, 1, 1)
    e, m = ext[0], ext[1]
    half_e, half_m = 0.5 * e, 0.5 * m
    centre = SURFACE + (half_e * spread(m) + half_m * spread(e))
    ext[3] = centre
    bound = jnp.max(2.0 * centre[:rows, :cols] - SURFACE, axis=0, keepdims=True)
    local = bound[:, :128]
    for start in range(128, cols, 128):
        local = jnp.maximum(local, bound[:, start : start + 128])
    maxima[0] = local

    def tell(i):
        pltpu.make_async_remote_copy(
            src_ref=maxima.at[0],
            dst_ref=maxima.at[i],
            send_sem=max_send,
            recv_sem=max_recv,
            device_id=peer(i),
            device_id_type=MESH,
        ).start()

    for_peers(tell)
    others = maxima.at[pl.ds(1, peers - 1)]

    carry = lax.fori_loop(steps // 2, steps, forward, carry)
    for k in range(steps * GROUP, levels):
        coupling = zero
        if k < levels - 1:
            coupling = jnp.where(k + 1 < wet_ref[...], cond[k].astype(jnp.float32), 0.0)
        carry = eliminate(k, carry, coupling)

    ext[2, rows : rows + 4, :cols] = land_edge[0, 1, 8:]
    ext[2, rows + 4 :, :cols] = land_edge[0, 0, 8:]
    widen_sides(0, 2, 2)

    e, m, residual, centre = ext[0], ext[1], ext[2], ext[3]
    half_e, half_m = 0.5 * e, 0.5 * m

    def operate(v):
        return centre * v - (half_e * spread(m * v) + half_m * spread(e * v))

    once = operate(residual)
    twice = operate(once)
    thrice = operate(twice)

    end_halo(0)
    pltpu.make_async_copy(others, others, max_send).wait()
    pltpu.make_async_copy(others, others, max_recv).wait()
    top = jnp.max(jnp.max(maxima[...], axis=0), axis=1, keepdims=True)

    theta = 0.5 * (top + SURFACE)
    delta = 0.5 * (top - SURFACE)
    sigma = theta / delta
    by_theta = 1.0 / theta
    direction = residual * by_theta
    recur = 1.0 / sigma
    result = jnp.zeros_like(residual)
    for step in range(ITERS):
        result = result + direction
        if step == 0:
            image, image_2 = once * by_theta, twice * by_theta
            image_3 = thrice * by_theta
        elif step == 1:
            image, image_2 = keep * image + gain * lead, keep * image_2 + gain * lead_2
        elif step == 2:
            image = keep * image + gain * lead
        else:
            image = operate(direction)
        residual = residual - image
        if step == 0:
            lead, lead_2 = once - image_2, twice - image_3
        elif step == 1:
            lead = lead - image_2
        recur_next = 1.0 / (2.0 * sigma - recur)
        keep, gain = recur_next * recur, 2.0 * recur_next / delta
        direction = keep * direction + gain * residual
        recur = recur_next
    height_ref[...] = (result + direction)[:rows, :cols]


def finish(ratios, values, height, heat_out, height_out, heat, sem):
    levels, rows, cols = values.shape
    parts = sem.shape[0] - 1
    per = levels // parts
    puts = [pltpu.make_async_copy(height, height_out, sem.at[parts])]
    puts[0].start()
    carry = jnp.zeros((rows, cols), jnp.float32)
    for part in reversed(range(parts)):
        for k in reversed(range(part * per, (part + 1) * per)):
            carry = values[k] + ratios[k] * carry
            heat[k] = carry
        span = pl.ds(part * per, per)
        puts.append(pltpu.make_async_copy(heat.at[span], heat_out.at[span], sem.at[part]))
        puts[-1].start()
    for put in puts:
        put.wait()


def local(n_row, n_col, heat, cond, spacing, wet, water, depth):
    levels, rows, cols = heat.shape
    f32 = jnp.float32
    parts = 6
    vmem = pl.BlockSpec(memory_space=pltpu.VMEM)
    hbm = pl.BlockSpec(memory_space=pltpu.HBM)
    dma = pltpu.SemaphoreType.DMA
    column = jax.ShapeDtypeStruct((levels, rows, cols), f32)
    surface = jax.ShapeDtypeStruct((rows, cols), f32)
    held = [
        pltpu.with_memory_space_constraint(x, pltpu.HBM)
        for x in (heat, cond, spacing, wet, water, depth)
    ]
    ratios, values, height = pl.pallas_call(
        functools.partial(kernel, n_row, n_col),
        out_shape=(column, column, surface),
        in_specs=[hbm] * 6,
        out_specs=(vmem, vmem, vmem),
        scratch_shapes=[
            pltpu.VMEM((levels, rows, cols), heat.dtype),
            pltpu.VMEM((levels - 1, rows, cols), cond.dtype),
            pltpu.SMEM((levels,), f32),
            pltpu.VMEM((rows, cols), wet.dtype),
            pltpu.VMEM((rows, cols), water.dtype),
            pltpu.VMEM((rows, cols), f32),
            pltpu.VMEM((4, rows + 8, cols + 128), f32),
            pltpu.VMEM((1, 2, 12, cols), f32),
            pltpu.VMEM((1, 2, 8, 128), f32),
            pltpu.VMEM((1, 2, 12, cols), f32),
            pltpu.VMEM((1, 6, 8, 128), f32),
            pltpu.VMEM((n_row * n_col, 1, 128), f32),
            dma((6,)),
            dma((1, 8)),
            dma((1, 8)),
            dma(()),
            dma(()),
        ],
        compiler_params=pltpu.CompilerParams(
            collective_id=0, has_side_effects=True, vmem_limit_bytes=GRANT
        ),
    )(*held)
    return pl.pallas_call(
        finish,
        out_shape=(column, surface),
        in_specs=[vmem, vmem, vmem],
        out_specs=(hbm, hbm),
        scratch_shapes=[pltpu.VMEM((levels, rows, cols), f32), dma((parts + 1,))],
        compiler_params=pltpu.CompilerParams(has_side_effects=True, vmem_limit_bytes=GRANT),
    )(ratios, values, height)


def solution(mesh):
    placed = (
        P(None, "row", "col"),
        P(None, "row", "col"),
        P(),
        P("row", "col"),
        P("row", "col"),
        P("row", "col"),
    )
    return jax.shard_map(
        functools.partial(local, mesh.shape["row"], mesh.shape["col"]),
        mesh=mesh,
        in_specs=placed,
        out_specs=(P(None, "row", "col"), P("row", "col")),
        check_vma=False,
    )
```

```python
import functools
import math

import jax
import jax.numpy as jnp
from jax import lax
from jax.experimental import pallas as pl
from jax.experimental.pallas import tpu as pltpu
from jax.sharding import PartitionSpec as P

ITERS = 4
SURFACE = 0.5
MESH = pl.DeviceIdType.MESH
GROUP = 4
GRANT = 32 * 1024 * 1024
SLOT = 8


def spread(field):
    rows, lanes = field.shape
    t = pltpu.roll(field, 1, 0) + pltpu.roll(field, rows - 1, 0)
    h = field + 0.5 * t
    return t + (pltpu.roll(h, 1, 1) + pltpu.roll(h, lanes - 1, 1))


def shift(block, by):
    lanes = block.shape[1]
    by = by % lanes
    return block if by == 0 else pltpu.roll(block, by, 1)


def pack_west(blocks):
    lane = lax.broadcasted_iota(jnp.int32, blocks[0].shape, 1)
    out = blocks[0]
    for slot in range(1, len(blocks)):
        out = jnp.where(lane >= SLOT * slot, shift(blocks[slot], SLOT * slot), out)
    return out


def pack_east(blocks):
    lane = lax.broadcasted_iota(jnp.int32, blocks[0].shape, 1)
    out = blocks[0]
    for slot in range(1, len(blocks)):
        out = jnp.where(lane < 128 - SLOT * slot, shift(blocks[slot], -SLOT * slot), out)
    return out


def kernel(
    n_row,
    n_col,
    heat_hbm,
    cond_hbm,
    spacing_hbm,
    wet_hbm,
    water_hbm,
    depth_hbm,
    ratios,
    values,
    height_ref,
    heat,
    cond,
    spacing,
    wet_ref,
    water_ref,
    depth_ref,
    ext,
    edge,
    side,
    land_edge,
    land_side,
    maxima,
    in_sem,
    send_sem,
    recv_sem,
    max_send,
    max_recv,
):
    levels, rows, cols = heat.shape
    half = cols - 128
    tiles = rows // 8
    row, col = lax.axis_index("row"), lax.axis_index("col")
    north, south = row > 0, row < n_row - 1
    up, down = lax.rem(row + n_row - 1, n_row), lax.rem(row + 1, n_row)
    west, east = lax.rem(col + n_col - 1, n_col), lax.rem(col + 1, n_col)

    pairs = (
        (water_hbm, water_ref),
        (depth_hbm, depth_ref),
        (wet_hbm, wet_ref),
        (spacing_hbm, spacing),
        (heat_hbm, heat),
        (cond_hbm, cond),
    )
    gets = [pltpu.make_async_copy(a, b, in_sem.at[i]) for i, (a, b) in enumerate(pairs)]
    for get in gets:
        get.start()

    barrier = pltpu.get_barrier_semaphore()

    def greet(r, c):
        pl.semaphore_signal(barrier, inc=1, device_id=(r, c), device_id_type=MESH)

    def peer(i):
        return lax.rem(row + i // n_col, n_row), lax.rem(col + lax.rem(i, n_col), n_col)

    peers = n_row * n_col

    def for_peers(act):
        if peers <= 64:
            for i in range(1, peers):
                act(jnp.int32(i))
        else:
            lax.fori_loop(1, peers, lambda i, none: (act(i), none)[1], None)

    for_peers(lambda i: greet(*peer(i)))

    @pl.when(jnp.logical_not(north))
    def _():
        for kind in range(1):
            for place in (2, 3):
                land_side[kind, place] = jnp.zeros((8, 128), jnp.float32)
            land_edge[kind, 0] = jnp.zeros((12, cols), jnp.float32)

    @pl.when(jnp.logical_not(south))
    def _():
        for kind in range(1):
            for place in (4, 5):
                land_side[kind, place] = jnp.zeros((8, 128), jnp.float32)
            land_edge[kind, 1] = jnp.zeros((12, cols), jnp.float32)

    def halo_copies(kind):
        def remote(src, dst, slot, target):
            return pltpu.make_async_remote_copy(
                src_ref=src,
                dst_ref=dst,
                send_sem=send_sem.at[kind, slot],
                recv_sem=recv_sem.at[kind, slot],
                device_id=target,
                device_id_type=MESH,
            )

        from_west, from_east = side.at[kind, 0], side.at[kind, 1]
        upper, lower = pl.ds(0, 4), pl.ds(4, 4)

        def corner(src, place, rows_sent, slot, target):
            return remote(
                src.at[rows_sent], land_side.at[kind, place, rows_sent], slot, target
            )

        northward = (
            remote(edge.at[kind, 0], land_edge.at[kind, 1], 0, (up, col)),
            corner(from_west, 5, upper, 1, (up, west)),
            corner(from_east, 4, upper, 2, (up, east)),
        )
        southward = (
            remote(edge.at[kind, 1], land_edge.at[kind, 0], 3, (down, col)),
            corner(from_west, 3, lower, 4, (down, west)),
            corner(from_east, 2, lower, 5, (down, east)),
        )
        sideways = (
            remote(from_west, land_side.at[kind, 1], 6, (row, west)),
            remote(from_east, land_side.at[kind, 0], 7, (row, east)),
        )
        return northward, southward, sideways

    def start_halo(kind):
        northward, southward, sideways = halo_copies(kind)

        @pl.when(north)
        def _():
            for copy in northward:
                copy.start()

        @pl.when(south)
        def _():
            for copy in southward:
                copy.start()

        for copy in sideways:
            copy.start()

    def wait_halo(kind):
        northward, southward, sideways = halo_copies(kind)

        @pl.when(south)
        def _():
            for copy in northward:
                copy.wait_recv()

        @pl.when(north)
        def _():
            for copy in southward:
                copy.wait_recv()

        for copy in sideways:
            copy.wait_recv()

    def end_halo(kind):
        northward, southward, sideways = halo_copies(kind)

        @pl.when(north)
        def _():
            for copy in northward:
                copy.wait_send()

        @pl.when(south)
        def _():
            for copy in southward:
                copy.wait_send()

        for copy in sideways:
            copy.wait_send()

    def stage_sides(kind, fields):
        blocks = [f[8 * t : 8 * t + 8, :128] for f in fields for t in range(tiles)]
        side[kind, 0] = pack_west(blocks)
        blocks = [f[8 * t : 8 * t + 8, half:] for f in fields for t in range(tiles)]
        side[kind, 1] = pack_east(blocks)

    sub_c = lax.broadcasted_iota(jnp.int32, (8, 128), 0)
    lane_c = lax.broadcasted_iota(jnp.int32, (8, 128), 1)

    def widen_sides(kind, slot, target):
        w, e = land_side[kind, 0], land_side[kind, 1]
        a_w = jnp.concatenate([land_side[kind, 4, :4], land_side[kind, 2, 4:]], axis=0)
        a_e = jnp.concatenate([land_side[kind, 5, :4], land_side[kind, 3, 4:]], axis=0)
        for t in range(tiles):
            by = SLOT * (slot * tiles + t)
            ext[target, pl.ds(8 * t, 8), cols:] = jnp.where(lane_c < 64, shift(e, -by), shift(w, by))
        first, last = SLOT * slot * tiles, SLOT * (slot * tiles + tiles - 1)
        above = jnp.where(lane_c < 64, shift(a_e, -last), shift(a_w, last))
        below = jnp.where(lane_c < 64, shift(a_e, -first), shift(a_w, first))
        ext[target, rows:, cols:] = jnp.where(sub_c < 4, below, above)

    gets[0].wait()
    gets[1].wait()
    mask = water_ref[...].astype(jnp.float32)
    masked_depth = mask * depth_ref[...]
    ext[0, :rows, :cols] = masked_depth
    ext[1, :rows, :cols] = mask
    sub8 = lax.broadcasted_iota(jnp.int32, (8, cols), 0)
    for get in gets[2:5]:
        get.wait()
    wet = wet_ref[...]

    def add_levels(step, total):
        for j in range(GROUP):
            k = step * GROUP + j
            total = total + jnp.where(k < wet, spacing[k] * heat[k].astype(jnp.float32), 0.0)
        return total

    zero = jnp.zeros((rows, cols), jnp.float32)
    total = lax.fori_loop(0, levels // GROUP, add_levels, zero)
    forcing = mask * total / math.sqrt(levels)
    ext[2, :rows, :cols] = forcing
    edge[0, 0, :8] = jnp.where(sub8 < 4, masked_depth[:8], pltpu.roll(mask[:8], 4, 0))
    edge[0, 0, 8:] = forcing[:4]
    edge[0, 1, :8] = jnp.where(
        sub8 >= 4, masked_depth[rows - 8 :], pltpu.roll(mask[rows - 8 :], 4, 0)
    )
    edge[0, 1, 8:] = forcing[rows - 4 :]
    stage_sides(0, (masked_depth, mask, forcing))
    pl.semaphore_wait(barrier, peers - 1)
    start_halo(0)

    gets[5].wait()

    def eliminate(k, carry, coupling):
        ratio, value, above = carry
        inverse = 1.0 / (spacing[k] + coupling + above * (1.0 - ratio))
        source = spacing[k] * heat[k].astype(jnp.float32)
        ratio = coupling * inverse
        value = (source + above * value) * inverse
        ratios[k] = ratio
        values[k] = value
        return ratio, value, coupling

    def forward(step, carry):
        for j in range(GROUP):
            k = step * GROUP + j
            coupling = jnp.where(k + 1 < wet_ref[...], cond[k].astype(jnp.float32), 0.0)
            carry = eliminate(k, carry, coupling)
        return carry

    steps = (levels - 1) // GROUP
    carry = lax.fori_loop(0, 3 * steps // 4, forward, (zero, zero, zero))

    wait_halo(0)
    from_n, from_s = land_edge[0, 0, :8], land_edge[0, 1, :8]
    ext[0, rows:, :cols] = jnp.where(sub8 < 4, from_s, from_n)
    ext[1, rows:, :cols] = pltpu.roll(jnp.where(sub8 >= 4, from_s, from_n), 4, 0)
    widen_sides(0, 0, 0)
    widen_sides(0, 1, 1)
    e, m = ext[0], ext[1]
    half_e, half_m = 0.5 * e, 0.5 * m
    centre = SURFACE + (half_e * spread(m) + half_m * spread(e))
    ext[3] = centre
    bound = jnp.max(2.0 * centre[:rows, :cols] - SURFACE, axis=0, keepdims=True)
    local = bound[:, :128]
    for start in range(128, cols, 128):
        local = jnp.maximum(local, bound[:, start : start + 128])
    maxima[0] = local

    def tell(i):
        pltpu.make_async_remote_copy(
            src_ref=maxima.at[0],
            dst_ref=maxima.at[i],
            send_sem=max_send,
            recv_sem=max_recv,
            device_id=peer(i),
            device_id_type=MESH,
        ).start()

    for_peers(tell)
    others = maxima.at[pl.ds(1, peers - 1)]

    carry = lax.fori_loop(3 * steps // 4, steps, forward, carry)
    for k in range(steps * GROUP, levels):
        coupling = zero
        if k < levels - 1:
            coupling = jnp.where(k + 1 < wet_ref[...], cond[k].astype(jnp.float32), 0.0)
        carry = eliminate(k, carry, coupling)

    ext[2, rows : rows + 4, :cols] = land_edge[0, 1, 8:]
    ext[2, rows + 4 :, :cols] = land_edge[0, 0, 8:]
    widen_sides(0, 2, 2)

    e, m, residual, centre = ext[0], ext[1], ext[2], ext[3]
    half_e, half_m = 0.5 * e, 0.5 * m

    def operate(v):
        return centre * v - (half_e * spread(m * v) + half_m * spread(e * v))

    once = operate(residual)
    twice = operate(once)
    thrice = operate(twice)

    end_halo(0)
    pltpu.make_async_copy(others, others, max_send).wait()
    pltpu.make_async_copy(others, others, max_recv).wait()
    top = jnp.max(jnp.max(maxima[...], axis=0), axis=1, keepdims=True)

    theta = 0.5 * (top + SURFACE)
    delta = 0.5 * (top - SURFACE)
    sigma = theta / delta
    by_theta = 1.0 / theta
    direction = residual * by_theta
    recur = 1.0 / sigma
    result = jnp.zeros_like(residual)
    for step in range(ITERS):
        result = result + direction
        if step == 0:
            image, image_2 = once * by_theta, twice * by_theta
            image_3 = thrice * by_theta
        elif step == 1:
            image, image_2 = keep * image + gain * lead, keep * image_2 + gain * lead_2
        elif step == 2:
            image = keep * image + gain * lead
        else:
            image = operate(direction)
        residual = residual - image
        if step == 0:
            lead, lead_2 = once - image_2, twice - image_3
        elif step == 1:
            lead = lead - image_2
        recur_next = 1.0 / (2.0 * sigma - recur)
        keep, gain = recur_next * recur, 2.0 * recur_next / delta
        direction = keep * direction + gain * residual
        recur = recur_next
    height_ref[...] = (result + direction)[:rows, :cols]


def finish(ratios, values, height, heat_out, height_out, heat, sem):
    levels, rows, cols = values.shape
    parts = sem.shape[0] - 1
    per = levels // parts
    puts = [pltpu.make_async_copy(height, height_out, sem.at[parts])]
    puts[0].start()
    carry = jnp.zeros((rows, cols), jnp.float32)
    for part in reversed(range(parts)):
        for k in reversed(range(part * per, (part + 1) * per)):
            carry = values[k] + ratios[k] * carry
            heat[k] = carry
        span = pl.ds(part * per, per)
        puts.append(pltpu.make_async_copy(heat.at[span], heat_out.at[span], sem.at[part]))
        puts[-1].start()
    for put in puts:
        put.wait()


def local(n_row, n_col, heat, cond, spacing, wet, water, depth):
    levels, rows, cols = heat.shape
    f32 = jnp.float32
    parts = 6
    vmem = pl.BlockSpec(memory_space=pltpu.VMEM)
    hbm = pl.BlockSpec(memory_space=pltpu.HBM)
    dma = pltpu.SemaphoreType.DMA
    column = jax.ShapeDtypeStruct((levels, rows, cols), f32)
    surface = jax.ShapeDtypeStruct((rows, cols), f32)
    held = [
        pltpu.with_memory_space_constraint(x, pltpu.HBM)
        for x in (heat, cond, spacing, wet, water, depth)
    ]
    ratios, values, height = pl.pallas_call(
        functools.partial(kernel, n_row, n_col),
        out_shape=(column, column, surface),
        in_specs=[hbm] * 6,
        out_specs=(vmem, vmem, vmem),
        scratch_shapes=[
            pltpu.VMEM((levels, rows, cols), heat.dtype),
            pltpu.VMEM((levels - 1, rows, cols), cond.dtype),
            pltpu.SMEM((levels,), f32),
            pltpu.VMEM((rows, cols), wet.dtype),
            pltpu.VMEM((rows, cols), water.dtype),
            pltpu.VMEM((rows, cols), f32),
            pltpu.VMEM((4, rows + 8, cols + 128), f32),
            pltpu.VMEM((1, 2, 12, cols), f32),
            pltpu.VMEM((1, 2, 8, 128), f32),
            pltpu.VMEM((1, 2, 12, cols), f32),
            pltpu.VMEM((1, 6, 8, 128), f32),
            pltpu.VMEM((n_row * n_col, 1, 128), f32),
            dma((6,)),
            dma((1, 8)),
            dma((1, 8)),
            dma(()),
            dma(()),
        ],
        compiler_params=pltpu.CompilerParams(
            collective_id=0, has_side_effects=True, vmem_limit_bytes=GRANT
        ),
    )(*held)
    return pl.pallas_call(
        finish,
        out_shape=(column, surface),
        in_specs=[vmem, vmem, vmem],
        out_specs=(hbm, hbm),
        scratch_shapes=[pltpu.VMEM((levels, rows, cols), f32), dma((parts + 1,))],
        compiler_params=pltpu.CompilerParams(has_side_effects=True, vmem_limit_bytes=GRANT),
    )(ratios, values, height)


def solution(mesh):
    placed = (
        P(None, "row", "col"),
        P(None, "row", "col"),
        P(),
        P("row", "col"),
        P("row", "col"),
        P("row", "col"),
    )
    return jax.shard_map(
        functools.partial(local, mesh.shape["row"], mesh.shape["col"]),
        mesh=mesh,
        in_specs=placed,
        out_specs=(P(None, "row", "col"), P("row", "col")),
        check_vma=False,
    )
```
